128 devices in a mesh: gy: 8 (over y, core), gx: 16 (over x, z).
Axes of the slice: x: 4, y: 4, z: 4, core: 2. Of those that a mesh axis runs over, the one named last changes fastest.
Arguments:
- features: bfloat16 [1024, 512, 128], P(('gy', 'gx')), may hold values from -6 to 6
- links: int32 [1024, 3], P(('gy', 'gx')), may hold values 0 or 1
- block_slot: int32 [1024], P(('gy', 'gx')), may hold values from 0 to 31, as said below
- block_level: int32 [1024], P(('gy', 'gx')), may hold values from 0 to 3
- slot_column: int32 [128, 32], P(('gy', 'gx')), may hold values from 0 to 31
- conv_first: bfloat16 [7, 128, 128], replicated, may hold values from -0.1875 to 0.1875
- conv_second: bfloat16 [7, 128, 128], replicated, may hold values from -0.1875 to 0.1875
- height_w: bfloat16 [4, 1024, 256], replicated, may hold values from -0.1875 to 0.1875
- plane_first: bfloat16 [3, 3, 256, 256], replicated, may hold values from -0.125 to 0.125
- plane_second: bfloat16 [3, 3, 256, 256], replicated, may hold values from -0.125 to 0.125
Outputs:
- bev_out: bfloat16 [512, 512, 256], P('gy', 'gx')
The draws below stay inside these ranges and needn't reach their ends.
Inputs may be any that keep to these rules, and one draw needn't show every extreme that they name: No two blocks of one device have both the same block_slot and the same block_level. At most 4 blocks of one device have the same block_slot // 2, and every device has exactly 4 such blocks for some value.
All inputs are finite; a program needn't handle non-finite values. No bound on the sum of `links` on one device may be relied on, other than what follows from the above.
Results may differ from the reference program's by a relative error of at most 0.0065.
Values may be sent and summed in bfloat16 or wider, within the bound.
A program may use at most 64 MiB of HBM per device.

```python
import jax
import jax.numpy as jnp
from jax import lax

C = 128
BEV_C = 256
EDGE = 8
BLOCK_DEV = 8
STRIDE_Y = 8
LEVELS = 4
CAP = 2
TILE_BR = 8
TILE_BC = 4
BLOCKS = 1024
SLOTS = 32
COLS = 32
MAP_R = 512
MAP_C = 512
N_GY = 8
N_GX = 16
DEVICES = 128


def choose_cells(key):
    base = jax.random.fold_in(key, 7103)
    cell_total = SLOTS * LEVELS
    tile_total = SLOTS // CAP

    def one_device(device):
        device_key = jax.random.fold_in(base, device)
        key_home, key_score, key_order, key_shift = jax.random.split(device_key, 4)
        cell = jnp.arange(cell_total, dtype=jnp.int32)
        tile = cell // (CAP * LEVELS)
        level = cell % LEVELS
        tile_ids = jnp.arange(tile_total, dtype=jnp.int32)
        start_level = jax.random.randint(key_shift, (tile_total,), 0, LEVELS)
        start_level = jnp.where((device == 0) & (tile_ids == tile_total - 1), 0, start_level).astype(jnp.int32)
        eligible = (level - start_level[tile]) % LEVELS < 2
        home = jax.random.randint(key_home, (), 0, tile_total)
        middle = (tile >= tile_total // 4) & (tile < tile_total - tile_total // 4)
        score = jax.random.randint(key_score, (cell_total,), 0, 1024) + 768 * middle.astype(jnp.int32)
        forced = (tile == home) & eligible | (device == 0) & (cell == cell_total - LEVELS)
        score = score + 100000 * forced.astype(jnp.int32) - 200000 * (1 - eligible.astype(jnp.int32))
        score = score * cell_total + cell
        unused, picked = lax.top_k(score, BLOCK_DEV)
        order = jax.random.permutation(key_order, BLOCK_DEV)
        return picked[order].astype(jnp.int32)
    return jax.vmap(one_device)(jnp.arange(DEVICES, dtype=jnp.int32)).reshape(-1)


def draw_block_slot(key, part):
    return (choose_cells(key) // LEVELS).astype(jnp.int32)


def draw_block_level(key, part):
    return (choose_cells(key) % LEVELS).astype(jnp.int32)


def plant(values, stream_key, low, largest):
    extent = values.shape
    index_at = [jax.random.randint(jax.random.fold_in(stream_key, axis), (), 0, extent[axis]) for axis in range(len(extent))]
    values = values.at[tuple(index_at)].set(low)
    longest = extent.index(max(extent))
    index_at[longest] = (index_at[longest] + 1) % extent[longest]
    return values.at[tuple(index_at)].set(largest)


def levels(rng, extent, pieces, least, high):
    def one(axis_at, shards_of):
        draws = jax.random.uniform(jax.random.fold_in(jax.random.fold_in(rng, 6), axis_at), (shards_of,), jnp.float32, least / len(pieces), high / len(pieces))
        return jnp.repeat(jnp.exp(draws), extent[axis_at] // shards_of).reshape((-1,) + (1,) * (len(extent) - axis_at - 1))

    factor_of = one(*pieces[0])
    for cut in pieces[1:]:
        factor_of = factor_of * one(*cut)
    return factor_of


def gaussian(own_key, dims, deviation, bound, shards=(), kind=jnp.bfloat16):
    array = deviation * jax.random.normal(own_key, dims, jnp.float32)
    if shards:
        array = array * levels(own_key, dims, shards, -0.22, 0.18)
    return jnp.clip(array, -bound, bound).astype(kind)


def setup_inputs(seed: int = 0) -> dict:
    streams_of = jax.random.split(jax.random.key(seed), 11)
    return {
        "features": gaussian(streams_of[0], (BLOCKS, EDGE**3, C), 1.0, 6.0, ((0, 128),)),
        "links": plant((jax.random.randint(streams_of[1], (BLOCKS, 3), 0, 4) < 3).astype(jnp.int32), jax.random.fold_in(streams_of[1], 1), 0, 1),
        "block_slot": draw_block_slot(jax.random.fold_in(streams_of[10], 71), 0),
        "block_level": draw_block_level(jax.random.fold_in(streams_of[10], 71), 0),
        "slot_column": plant(jax.random.randint(streams_of[4], (DEVICES, SLOTS), 0, COLS), jax.random.fold_in(streams_of[4], 1), 0, COLS - 1).astype(jnp.int32),
        "conv_first": gaussian(streams_of[5], (7, C, C), (7 * C) ** -0.5, 0.1875),
        "conv_second": gaussian(streams_of[6], (7, C, C), (7 * C) ** -0.5, 0.1875),
        "height_w": gaussian(streams_of[7], (LEVELS, EDGE * C, BEV_C), (EDGE * C) ** -0.5, 0.1875),
        "plane_first": gaussian(streams_of[8], (3, 3, BEV_C, BEV_C), (9 * BEV_C) ** -0.5, 0.125),
        "plane_second": gaussian(streams_of[9], (3, 3, BEV_C, BEV_C), (9 * BEV_C) ** -0.5, 0.125),
    }


def block_ghosts(blocks, links):
    block_count = blocks.shape[0]
    strides = (1, STRIDE_Y, BLOCK_DEV)
    ghost_plus = []
    ghost_minus = []
    for axis_num in range(3):
        upper = lax.index_in_dim(blocks, EDGE - 1, axis_num + 1, keepdims=False)
        lower = lax.index_in_dim(blocks, 0, axis_num + 1, keepdims=False)
        keeping = links[:, axis_num].astype(blocks.dtype)[:, None, None, None]
        upper = upper * keeping
        stride = strides[axis_num]
        padding = jnp.zeros((stride,) + upper.shape[1:], blocks.dtype)
        ghost_plus.append(jnp.concatenate([lower[stride:], padding], 0) * keeping)
        ghost_minus.append(jnp.concatenate([padding, upper[:block_count - stride]], 0))
    return ghost_plus, ghost_minus


def seven_taps(blocks, ghost_plus, ghost_minus, weights):
    channels = blocks.shape[-1]
    result = jnp.dot(blocks.reshape(-1, channels), weights[0], preferred_element_type=jnp.float32)
    for axis_num in range(3):
        axis = axis_num + 1
        upward = jnp.concatenate([lax.slice_in_dim(blocks, 1, EDGE, axis=axis), jnp.expand_dims(ghost_plus[axis_num], axis)], axis)
        downward = jnp.concatenate([jnp.expand_dims(ghost_minus[axis_num], axis), lax.slice_in_dim(blocks, 0, EDGE - 1, axis=axis)], axis)
        result = result + jnp.dot(upward.reshape(-1, channels), weights[1 + 2 * axis_num], preferred_element_type=jnp.float32)
        result = result + jnp.dot(downward.reshape(-1, channels), weights[2 + 2 * axis_num], preferred_element_type=jnp.float32)
    return result.reshape(blocks.shape)


def plane_conv(padded, kernel, rows_out, cols_out):
    result = jnp.zeros((rows_out * cols_out, kernel.shape[3]), jnp.float32)
    for row_off in range(3):
        for col_off in range(3):
            window = padded[row_off:row_off + rows_out, col_off:col_off + cols_out].reshape(rows_out * cols_out, -1)
            result = result + jnp.dot(window, kernel[row_off, col_off], preferred_element_type=jnp.float32)
    return result.reshape(rows_out, cols_out, -1)


def reference(features, links, block_slot, block_level, slot_column, conv_first, conv_second, height_w, plane_first, plane_second):
    blocks = features.reshape(BLOCKS, EDGE, EDGE, EDGE, C)
    ghost_plus, ghost_minus = block_ghosts(blocks, links)
    hidden = jax.nn.relu(seven_taps(blocks, ghost_plus, ghost_minus, conv_first)).astype(jnp.bfloat16)
    ghost_plus, ghost_minus = block_ghosts(hidden, links)
    voxel = jax.nn.relu(blocks.astype(jnp.float32) + seven_taps(hidden, ghost_plus, ghost_minus, conv_second)).astype(jnp.bfloat16)
    grouped = voxel.reshape(DEVICES, BLOCK_DEV, EDGE * EDGE, EDGE * C)
    level_groups = block_level.reshape(DEVICES, BLOCK_DEV)

    def collapse(pair):
        group_rows, group_levels = pair
        chosen = jnp.take(height_w, group_levels, axis=0).astype(jnp.float32)
        return jnp.einsum("bpk,bkn->bpn", group_rows.astype(jnp.float32), chosen)

    lifted = lax.map(collapse, (grouped, level_groups)).reshape(BLOCKS, EDGE * EDGE, BEV_C)
    device_of = (jnp.arange(BLOCKS, dtype=jnp.int32) // BLOCK_DEV).astype(jnp.int32)
    tile_row = device_of // N_GX
    tile_col = block_slot // CAP
    column = slot_column[device_of, block_slot]
    block_row = tile_row * TILE_BR + column // TILE_BC
    block_col = tile_col * TILE_BC + column % TILE_BC
    target = (block_row * (N_GX * TILE_BC) + block_col).astype(jnp.int32)
    summed = jnp.zeros((N_GY * TILE_BR * N_GX * TILE_BC, EDGE * EDGE, BEV_C), jnp.float32).at[target].add(lifted)
    bev = summed.reshape(N_GY * TILE_BR, N_GX * TILE_BC, EDGE, EDGE, BEV_C).transpose(0, 2, 1, 3, 4)
    bev = bev.reshape(MAP_R, MAP_C, BEV_C).astype(jnp.bfloat16)
    padded = jnp.pad(bev, ((1, 1), (1, 1), (0, 0)))
    first = jax.nn.relu(plane_conv(padded, plane_first, MAP_R, MAP_C)).astype(jnp.bfloat16)
    padded = jnp.pad(first, ((1, 1), (1, 1), (0, 0)))
    return (plane_conv(padded, plane_second, MAP_R, MAP_C) + bev.astype(jnp.float32)).astype(jnp.bfloat16)
```

```python
import jax
import jax.numpy as jnp
from jax import lax
from jax.experimental import pallas as pl
from jax.experimental.pallas import tpu as pltpu
from jax.sharding import PartitionSpec as P

NY = 8
NX = 16
MESH = pl.DeviceIdType.MESH
F32 = jnp.float32
BF = jnp.bfloat16


def iota(shape, dim):
    return lax.broadcasted_iota(jnp.int32, shape, dim)


def shr(x, n):
    return lax.shift_right_logical(x, jnp.int32(n))


def onehot(cond):
    return jnp.where(cond, 1.0, 0.0).astype(BF)


def mm(a, b):
    return jnp.dot(a, b, preferred_element_type=F32)


def kernel(
    x_hbm, links, slot, level, ids_in, w1_hbm, w2_hbm, h_hbm, p1_hbm, p2_hbm,
    out,
    xv, w1, w2, hw, p1, p2,
    fa, fb, stage, ghost, astage, aghost,
    perm, up1, dn1, pick, spread,
    sbuf, rbuf, ids, idl,
    bev, first, cstage, cland, rstage, rland, kland,
    wsem, hsend, hrecv, asend, arecv, tsend, trecv, isend, irecv, msend, mrecv,
):
    gy = lax.axis_index("gy")
    gx = lax.axis_index("gx")
    nxt = ((gy + (gx + 1) // NX) % NY, (gx + 1) % NX)
    prv = ((gy + NY - 1 + (gx + NX - 1) // NX) % NY, (gx + NX - 1) % NX)
    north, south = (gy + NY - 1) % NY, (gy + 1) % NY
    west, east = (gx + NX - 1) % NX, (gx + 1) % NX

    loads = [
        pltpu.make_async_copy(s, d, wsem.at[n])
        for n, (s, d) in enumerate(
            [(x_hbm, xv), (w1_hbm, w1), (w2_hbm, w2), (h_hbm, hw), (p1_hbm, p1), (p2_hbm, p2)]
        )
    ]
    for load in loads:
        load.start()

    barrier = pltpu.get_barrier_semaphore()

    def hello(where):
        pl.semaphore_signal(barrier, inc=1, device_id=where, device_id_type=MESH)

    hello(nxt)
    hello(prv)
    for v in (north, gy, south):
        for h in (west, gx, east):
            if v is gy and h is gx:
                continue
            hello((v, h))

    def greet(o, carry):
        hello((gy, (gx + o) % NX))
        return carry

    lax.fori_loop(1, NX, greet, 0)

    r = iota((256, 256), 0)
    q = iota((256, 256), 1)
    perm[...] = onehot(q == (r & 15) * 16 + shr(r, 4))
    up1[...] = onehot((q == r + 1) & ((r & 15) != 15))
    dn1[...] = onehot((q == r - 1) & ((r & 15) != 0))
    r = iota((16, 256), 0)
    q = iota((16, 256), 1)
    pick[0] = onehot(q == r * 16)
    pick[1] = onehot(q == r * 16 + 15)
    r = iota((256, 16), 0)
    q = iota((256, 16), 1)
    spread[0] = onehot(r == q * 16)
    spread[1] = onehot(r == q * 16 + 15)

    ids[...] = jnp.zeros((8, 128), F32)
    ids[0:1, 0:32] = ids_in[...].astype(F32)

    s16 = iota((16, 128), 0)

    def per_block(read, index):
        m = jnp.zeros((16, 128), F32)
        for i in range(8):
            m = jnp.where(index == i, read(i).astype(F32), m)
        return m

    m1 = per_block(lambda i: links[i, 1], shr(s16, 1))
    m2 = per_block(lambda i: links[i, 2], shr(s16, 1))
    ma = jnp.where((s16 & 1) == 0, 1.0, per_block(lambda i: links[i, 0], shr(s16, 1)))
    mb = jnp.where((s16 & 1) == 1, 1.0, per_block(lambda i: links[i, 0], shr(s16, 1) - 1))
    not_last = jnp.where((gx < NX - 1) | (gy < NY - 1), 1.0, 0.0).astype(F32)
    not_first = jnp.where((gx > 0) | (gy > 0), 1.0, 0.0).astype(F32)
    m1p = m1 * not_last
    m2p = m2 * not_last
    top = links[7, 0].astype(F32)

    def times(x, m):
        return (x.astype(F32) * m).astype(BF)

    def face_copy(ph, way, al):
        return pltpu.make_async_remote_copy(
            src_ref=stage.at[ph, way, al],
            dst_ref=ghost.at[ph, way, al],
            send_sem=hsend.at[ph, way, al],
            recv_sem=hrecv.at[ph, way, al],
            device_id=nxt if way else prv,
            device_id_type=MESH,
        )

    def end_copy(ph, way):
        return pltpu.make_async_remote_copy(
            src_ref=astage.at[ph, way],
            dst_ref=aghost.at[ph, way],
            send_sem=asend.at[ph, way],
            recv_sem=arecv.at[ph, way],
            device_id=nxt if way else prv,
            device_id_type=MESH,
        )

    def publish(ph, arr, al):
        stage[ph, 0, al, 0] = arr[al + 1, 1, 1:9]
        stage[ph, 0, al, 1] = arr[al + 1, 1:9, 1]
        stage[ph, 1, al, 0] = times(arr[al + 1, 8, 1:9], m1)
        stage[ph, 1, al, 1] = times(arr[al + 1, 1:9, 8], m2)
        face_copy(ph, 0, al).start()
        face_copy(ph, 1, al).start()

    def publish_end(ph, arr, way):
        for g in range(4):
            rows = arr[4 if way else 1, 1 + 2 * g : 3 + 2 * g, 1:9].reshape(256, 128)
            face = mm(pick[way], rows)
            if way:
                face = face * top
            astage[ph, way, g * 16 : g * 16 + 16] = face.astype(BF)
        end_copy(ph, way).start()

    def absorb(ph, arr, al):
        face_copy(ph, 0, al).wait_recv()
        face_copy(ph, 1, al).wait_recv()
        arr[al + 1, 9, 1:9] = times(ghost[ph, 0, al, 0], m1p)
        arr[al + 1, 1:9, 9] = times(ghost[ph, 0, al, 1], m2p)
        arr[al + 1, 0, 1:9] = times(ghost[ph, 1, al, 0], not_first)
        arr[al + 1, 1:9, 0] = times(ghost[ph, 1, al, 1], not_first)

    def absorb_ends(ph, arr):
        end_copy(ph, 0).wait_recv()
        end_copy(ph, 1).wait_recv()
        for g in range(4):
            bs = slice(1 + 2 * g, 3 + 2 * g)
            gs = slice(g * 16, g * 16 + 16)
            rows = mm(up1[...], arr[1, bs, 1:9].reshape(256, 128)).reshape(16, 16, 128) * ma
            end = mm(spread[1], aghost[ph, 0, gs]).reshape(16, 16, 128) * (top * not_last)
            arr[5, bs, 1:9] = (rows + end).astype(BF).reshape(2, 8, 16, 128)
            rows = mm(dn1[...], arr[4, bs, 1:9].reshape(256, 128)).reshape(16, 16, 128) * mb
            end = mm(spread[0], aghost[ph, 1, gs]).reshape(16, 16, 128) * not_first
            arr[0, bs, 1:9] = (rows + end).astype(BF).reshape(2, 8, 16, 128)

    def taps(arr, al, b0, nb):
        n = nb * 128
        win = [
            arr[al + 1, 1 + b0 : 1 + b0 + nb, 1:9],
            arr[al + 2, 1 + b0 : 1 + b0 + nb, 1:9],
            arr[al, 1 + b0 : 1 + b0 + nb, 1:9],
            arr[al + 1, 2 + b0 : 2 + b0 + nb, 1:9],
            arr[al + 1, b0 : b0 + nb, 1:9],
            arr[al + 1, 1 + b0 : 1 + b0 + nb, 2:10],
            arr[al + 1, 1 + b0 : 1 + b0 + nb, 0:8],
        ]
        return jnp.concatenate([w.reshape(n, 128) for w in win], axis=1)

    loads[0].wait()
    pl.semaphore_wait(barrier, 25)

    def send_ids(o, carry):
        pltpu.make_async_remote_copy(
            src_ref=ids,
            dst_ref=idl.at[gx],
            send_sem=isend,
            recv_sem=irecv,
            device_id=(gy, (gx + o) % NX),
            device_id_type=MESH,
        ).start()
        return carry

    def bring(t, carry):
        al = (t + 3) % 4
        for g in (0, 2):
            two = [
                xv[:, :, al, k * 16 : k * 16 + 16, :].reshape(256, 128) for k in (g, g + 1)
            ]
            moved = mm(perm[...], jnp.concatenate(two, axis=1)).astype(BF)
            for n in range(2):
                fa[al + 1, 1 + 2 * (g + n) : 3 + 2 * (g + n), 1:9] = moved[
                    :, n * 128 : n * 128 + 128
                ].reshape(2, 8, 16, 128)
        publish(0, fa, al)
        return carry

    lax.fori_loop(0, 4, bring, 0)
    publish_end(0, fa, 0)
    publish_end(0, fa, 1)
    lax.fori_loop(1, NX, send_ids, 0)
    idl[gx] = ids[...]

    loads[1].wait()
    absorb_ends(0, fa)

    def conv_one(t, carry):
        al = (t + 3) % 4
        absorb(0, fa, al)
        for b0 in (0, 4):
            h = mm(taps(fa, al, b0, 4), w1[...])
            fb[al + 1, 1 + b0 : 5 + b0, 1:9] = (
                jnp.maximum(h, 0.0).astype(BF).reshape(4, 8, 16, 128)
            )
        publish(1, fb, al)

        @pl.when(t == 0)
        def _():
            publish_end(1, fb, 1)

        @pl.when(t == 1)
        def _():
            publish_end(1, fb, 0)

        return carry

    lax.fori_loop(0, 4, conv_one, 0)

    lane = iota((1, 128), 1)
    slot_lane = jnp.zeros((1, 128), jnp.int32)
    for i in range(8):
        slot_lane = jnp.where((shr(lane, 1) & 7) == i, slot[i], slot_lane)
    k = iota((512, 128), 0)
    rho = iota((512, 128), 1)
    slot_mat = onehot(
        (shr(k, 4) == slot_lane) & ((shr(k, 1) & 7) == shr(rho, 4)) & ((k & 1) == (rho & 1))
    )
    row_block = shr(iota((128, 256), 0), 1) & 7
    row_level = jnp.zeros((128, 256), jnp.int32)
    for i in range(8):
        row_level = jnp.where(row_block == i, level[i], row_level)

    loads[2].wait()
    loads[3].wait()
    absorb_ends(1, fb)

    def column_copy(al, o):
        to = (gx + o) % NX
        return pltpu.make_async_remote_copy(
            src_ref=sbuf.at[al, to],
            dst_ref=rbuf.at[al, gx],
            send_sem=tsend.at[al],
            recv_sem=trecv.at[al],
            device_id=(gy, to),
            device_id_type=MESH,
        )

    def conv_two(t, carry):
        al = (t + 3) % 4
        absorb(1, fb, al)
        parts = []
        for b0 in (0, 4):
            v = mm(taps(fb, al, b0, 4), w2[...])
            v = v + fa[al + 1, 1 + b0 : 5 + b0, 1:9].reshape(512, 128).astype(F32)
            v = jnp.maximum(v, 0.0).astype(BF).reshape(4, 8, 16, 128)
            parts.append(
                jnp.concatenate([v[:, c].reshape(64, 128) for c in range(8)], axis=1)
            )
        rows = jnp.concatenate(parts, axis=0)
        lifted = jnp.zeros((128, 256), F32)
        for lv in range(4):
            lifted = jnp.where(row_level == lv, mm(rows, hw[lv]), lifted)
        high = lifted.astype(BF)
        low = (lifted - high.astype(F32)).astype(BF)
        sums = mm(slot_mat, high) + mm(slot_mat, low)
        sbuf[al] = sums.astype(BF).reshape(16, 32, 256)

        def send(o, c):
            column_copy(al, o).start()
            return c

        lax.fori_loop(1, NX, send, 0)
        rbuf[al, gx] = sbuf[al, gx]
        return carry

    lax.fori_loop(0, 4, conv_two, 0)

    pltpu.make_async_copy(idl.at[0:15], idl.at[0:15], irecv).wait()
    sel = onehot(iota((128, 512), 0) == 2 * gx + (shr(iota((128, 512), 1), 4) & 1))
    got = mm(idl[...].reshape(128, 128).astype(BF), sel)
    rr = iota((128, 512), 0)
    kk = iota((128, 512), 1)
    got = jnp.where(((rr & 7) == 0) & (shr(rr, 3) == shr(kk, 5)), got, 0.0)
    cid = jnp.sum(got, axis=0, keepdims=True)
    r = iota((512, 512), 0)
    k = iota((512, 512), 1)
    want = (shr(r, 1) & 7) * 4 + shr(r, 7)
    tile_mat = onehot(
        (cid == want.astype(F32)) & ((shr(r, 4) & 7) == (shr(k, 1) & 7)) & ((r & 1) == (k & 1))
    )

    def gather(t, carry):
        al = (t + 3) % 4
        pltpu.make_async_copy(rbuf.at[al, 0:15], rbuf.at[al, 0:15], trecv.at[al]).wait()
        tile = mm(tile_mat, rbuf[al].reshape(512, 256))
        bev[al + 2, 2:34] = tile.astype(BF).reshape(32, 16, 256)
        return carry

    lax.fori_loop(0, 4, gather, 0)

    cstage[0] = bev[2:6, 2:4]
    cstage[1] = bev[2:6, 32:34]
    for n in range(2):
        for g in range(2):
            xs = slice(2 + 16 * g, 18 + 16 * g)
            gs = slice(16 * g, 16 * g + 16)
            rstage[0, n, gs] = mm(pick[0], bev[2 + n, xs].reshape(256, 256)).astype(BF)
            rstage[1, n, gs] = mm(pick[1], bev[4 + n, xs].reshape(256, 256)).astype(BF)

    def rim(n, src, dst, where):
        return pltpu.make_async_remote_copy(
            src_ref=src,
            dst_ref=dst,
            send_sem=msend.at[n],
            recv_sem=mrecv.at[n],
            device_id=where,
            device_id_type=MESH,
        )

    rims = [
        rim(0, cstage.at[0], cland.at[0], (gy, west)),
        rim(1, cstage.at[1], cland.at[1], (gy, east)),
        rim(2, rstage.at[0], rland.at[0], (north, gx)),
        rim(3, rstage.at[1], rland.at[1], (south, gx)),
        rim(4, rstage.at[0, :, 0:16], kland.at[0], (north, west)),
        rim(5, rstage.at[0, :, 16:32], kland.at[1], (north, east)),
        rim(6, rstage.at[1, :, 0:16], kland.at[2], (south, west)),
        rim(7, rstage.at[1, :, 16:32], kland.at[3], (south, east)),
    ]
    for c in rims:
        c.start()
    has_n = jnp.where(gy > 0, 1.0, 0.0).astype(F32)
    has_s = jnp.where(gy < NY - 1, 1.0, 0.0).astype(F32)
    has_w = jnp.where(gx > 0, 1.0, 0.0).astype(F32)
    has_e = jnp.where(gx < NX - 1, 1.0, 0.0).astype(F32)
    for c in rims:
        c.wait_recv()
    bev[2:6, 34:36] = times(cland[0], has_e)
    bev[2:6, 0:2] = times(cland[1], has_w)
    r = iota((32, 16), 0)
    q = iota((32, 16), 1)
    at_start = [onehot((r == q * 16 + 15)), onehot((r == q * 16))]
    at_end = [onehot((r == (q - 14) * 16 + 15)), onehot((r == (q - 14) * 16))]
    for n in range(2):
        for way, src, dst, sh, there in ((0, 2 + n, 6 + n, up1, has_s), (1, 4 + n, n, dn1, has_n)):
            for g in range(2):
                xs = slice(2 + 16 * g, 18 + 16 * g)
                gs = slice(16 * g, 16 * g + 16)
                rows = mm(sh[...], bev[src, xs].reshape(256, 256))
                rows = rows + mm(spread[1 - way], rland[way, n, gs]) * there
                bev[dst, xs] = rows.astype(BF).reshape(16, 16, 256)
            rows = mm(sh[0:32, 0:32], bev[src, 0:2].reshape(32, 256))
            rows = rows + mm(at_end[way], kland[2 * way + 1, n]) * (there * has_w)
            bev[dst, 0:2] = rows.astype(BF).reshape(2, 16, 256)
            rows = mm(sh[0:32, 0:32], bev[src, 34:36].reshape(32, 256))
            rows = rows + mm(at_start[way], kland[2 * way, n]) * (there * has_e)
            bev[dst, 34:36] = rows.astype(BF).reshape(2, 16, 256)
    upper = iota((36, 16, 256), 1) < 8
    for n in range(3):
        bev[8 + n] = jnp.where(upper, bev[n].astype(F32), bev[5 + n].astype(F32)).astype(BF)

    loads[4].wait()

    def plane_one(t, carry):
        yl = t + 3 * (t // 4)
        win = [
            bev[yl + 1 + dy, dx : dx + 34].reshape(544, 256)
            for dy in range(3)
            for dx in range(3)
        ]
        f = mm(jnp.concatenate(win, axis=1), p1[...])
        first[t + 1, 0:34] = jnp.maximum(f, 0.0).astype(BF).reshape(34, 16, 256)
        return carry

    lax.fori_loop(0, 5, plane_one, 0)
    first[1:6, 0:1] = times(first[1:6, 0:1], has_w)
    first[1:6, 33:34] = times(first[1:6, 33:34], has_e)
    for x0, n in ((0, 16), (16, 16), (32, 2)):
        m = n * 16
        xs = slice(x0, x0 + n)
        edge = first[5, xs].reshape(m, 256).astype(F32)
        row = iota((m, 256), 0) & 15
        below = mm(up1[0:m, 0:m], first[1, xs].reshape(m, 256))
        below = jnp.where(row == 15, edge * has_s, below)
        above = mm(dn1[0:m, 0:m], first[4, xs].reshape(m, 256))
        above = jnp.where(row == 0, edge * has_n, above)
        first[0, xs] = above.astype(BF).reshape(n, 16, 256)
        first[5, xs] = below.astype(BF).reshape(n, 16, 256)

    loads[5].wait()

    def plane_two(yl, carry):
        win = [
            first[yl + dy, dx : dx + 32].reshape(512, 256) for dy in range(3) for dx in range(3)
        ]
        s = mm(jnp.concatenate(win, axis=1), p2[...])
        s = (s + bev[yl + 2, 2:34].reshape(512, 256).astype(F32)).astype(BF)
        for g in range(2):
            moved = mm(perm[...], s[256 * g : 256 * g + 256]).astype(BF)
            out[:, yl, 16 * g : 16 * g + 16, :] = moved.reshape(16, 16, 256)
        return carry

    lax.fori_loop(0, 4, plane_two, 0)

    for ph in range(2):
        for way in range(2):
            end_copy(ph, way).wait_send()
            for al in range(4):
                face_copy(ph, way, al).wait_send()
    for al in range(4):
        pltpu.make_async_copy(sbuf.at[al, 0:15], sbuf.at[al, 0:15], tsend.at[al]).wait()
    pltpu.make_async_copy(idl.at[0:15], idl.at[0:15], isend).wait()
    for c in rims:
        c.wait_send()


def local(
    features, links, block_slot, block_level, slot_column,
    conv_first, conv_second, height_w, plane_first, plane_second,
):
    hbm = pl.BlockSpec(memory_space=pl.ANY)
    smem = pl.BlockSpec(memory_space=pltpu.SMEM)
    vmem = pl.BlockSpec(memory_space=pltpu.VMEM)
    dma = pltpu.SemaphoreType.DMA
    out = pl.pallas_call(
        kernel,
        out_shape=jax.ShapeDtypeStruct((16, 4, 32, 256), BF),
        in_specs=[hbm, smem, smem, smem, vmem, hbm, hbm, hbm, hbm, hbm],
        out_specs=vmem,
        scratch_shapes=[
            pltpu.VMEM((8, 2, 4, 64, 128), BF),
            pltpu.VMEM((896, 128), BF),
            pltpu.VMEM((896, 128), BF),
            pltpu.VMEM((4, 1024, 256), BF),
            pltpu.VMEM((2304, 256), BF),
            pltpu.VMEM((2304, 256), BF),
            pltpu.VMEM((6, 10, 10, 16, 128), BF),
            pltpu.VMEM((6, 10, 10, 16, 128), BF),
            pltpu.VMEM((2, 2, 4, 2, 8, 16, 128), BF),
            pltpu.VMEM((2, 2, 4, 2, 8, 16, 128), BF),
            pltpu.VMEM((2, 2, 64, 128), BF),
            pltpu.VMEM((2, 2, 64, 128), BF),
            pltpu.VMEM((256, 256), BF),
            pltpu.VMEM((256, 256), BF),
            pltpu.VMEM((256, 256), BF),
            pltpu.VMEM((2, 16, 256), BF),
            pltpu.VMEM((2, 256, 16), BF),
            pltpu.VMEM((4, 16, 32, 256), BF),
            pltpu.VMEM((4, 16, 32, 256), BF),
            pltpu.VMEM((8, 128), F32),
            pltpu.VMEM((16, 8, 128), F32),
            pltpu.VMEM((11, 36, 16, 256), BF),
            pltpu.VMEM((6, 34, 16, 256), BF),
            pltpu.VMEM((2, 4, 2, 16, 256), BF),
            pltpu.VMEM((2, 4, 2, 16, 256), BF),
            pltpu.VMEM((2, 2, 32, 256), BF),
            pltpu.VMEM((2, 2, 32, 256), BF),
            pltpu.VMEM((4, 2, 16, 256), BF),
            dma((6,)),
            dma((2, 2, 4)),
            dma((2, 2, 4)),
            dma((2, 2)),
            dma((2, 2)),
            dma((4,)),
            dma((4,)),
            dma,
            dma,
            dma((8,)),
            dma((8,)),
        ],
        compiler_params=pltpu.CompilerParams(
            collective_id=0, has_side_effects=True, vmem_limit_bytes=56 * 2**20
        ),
    )(
        features.reshape(8, 2, 4, 64, 128),
        links,
        block_slot,
        block_level,
        slot_column,
        conv_first.reshape(896, 128),
        conv_second.reshape(896, 128),
        height_w,
        plane_first.reshape(2304, 256),
        plane_second.reshape(2304, 256),
    )
    return out.reshape(64, 32, 256)


def solution(mesh):
    in_specs = (
        P(("gy", "gx"), None, None),
        P(("gy", "gx"), None),
        P(("gy", "gx")),
        P(("gy", "gx")),
        P(("gy", "gx"), None),
        P(),
        P(),
        P(),
        P(),
        P(),
    )
    return jax.shard_map(
        local, mesh=mesh, in_specs=in_specs, out_specs=P("gy", "gx", None), check_vma=False
    )
```

```python
import jax
import jax.numpy as jnp
from jax import lax
from jax.experimental import pallas as pl
from jax.experimental.pallas import tpu as pltpu
from jax.sharding import PartitionSpec as P

NY = 8
NX = 16
MESH = pl.DeviceIdType.MESH
F32 = jnp.float32
BF = jnp.bfloat16


def iota(shape, dim):
    return lax.broadcasted_iota(jnp.int32, shape, dim)


def shr(x, n):
    return lax.shift_right_logical(x, jnp.int32(n))


def onehot(cond):
    return jnp.where(cond, 1.0, 0.0).astype(BF)


def mm(a, b):
    return jnp.dot(a, b, preferred_element_type=F32)


def kernel(
    x_hbm, links_hbm, slot_hbm, level_hbm, ids_hbm, w1_hbm, w2_hbm, h_hbm, p1_hbm,
    first, base,
    links, slot, level, ids_in, xv, w1, w2, hw, p1,
    fa, fb, stage, ghost, astage, aghost,
    perm, up1, dn1, pick, spread,
    sbuf, rbuf, ids, idl,
    bev, edge, cstage, cland, rstage, rland, kland,
    wsem, hsend, hrecv, asend, arecv, tsend, trecv, isend, irecv, msend, mrecv,
):
    gy = lax.axis_index("gy")
    gx = lax.axis_index("gx")
    nxt = ((gy + (gx + 1) // NX) % NY, (gx + 1) % NX)
    prv = ((gy + NY - 1 + (gx + NX - 1) // NX) % NY, (gx + NX - 1) % NX)
    north, south = (gy + NY - 1) % NY, (gy + 1) % NY
    west, east = (gx + NX - 1) % NX, (gx + 1) % NX

    loads = [
        pltpu.make_async_copy(s, d, wsem.at[n])
        for n, (s, d) in enumerate(
            [
                (x_hbm, xv), (w1_hbm, w1), (w2_hbm, w2), (h_hbm, hw), (p1_hbm, p1),
                (links_hbm, links), (slot_hbm, slot), (level_hbm, level), (ids_hbm, ids_in),
            ]
        )
    ]
    for load in loads:
        load.start()

    barrier = pltpu.get_barrier_semaphore()

    def hello(where):
        pl.semaphore_signal(barrier, inc=1, device_id=where, device_id_type=MESH)

    hello(nxt)
    hello(prv)
    for v in (north, gy, south):
        for h in (west, gx, east):
            if v is gy and h is gx:
                continue
            hello((v, h))

    def greet(o, carry):
        hello((gy, (gx + o) % NX))
        return carry

    lax.fori_loop(1, NX, greet, 0)

    r = iota((256, 256), 0)
    q = iota((256, 256), 1)
    perm[...] = onehot(q == (r & 15) * 16 + shr(r, 4))
    up1[...] = onehot((q == r + 1) & ((r & 15) != 15))
    dn1[...] = onehot((q == r - 1) & ((r & 15) != 0))
    r = iota((16, 256), 0)
    q = iota((16, 256), 1)
    pick[0] = onehot(q == r * 16)
    pick[1] = onehot(q == r * 16 + 15)
    r = iota((256, 16), 0)
    q = iota((256, 16), 1)
    spread[0] = onehot(r == q * 16)
    spread[1] = onehot(r == q * 16 + 15)

    for load in loads[5:]:
        load.wait()
    ids[...] = jnp.zeros((1, 128), F32)
    ids[0:1, 0:32] = ids_in[...].astype(F32)

    s16 = iota((16, 128), 0)

    def per_block(read, index):
        m = jnp.zeros((16, 128), F32)
        for i in range(8):
            m = jnp.where(index == i, read(i).astype(F32), m)
        return m

    m1 = per_block(lambda i: links[1, i], shr(s16, 1))
    m2 = per_block(lambda i: links[2, i], shr(s16, 1))
    ma = jnp.where((s16 & 1) == 0, 1.0, per_block(lambda i: links[0, i], shr(s16, 1)))
    mb = jnp.where((s16 & 1) == 1, 1.0, per_block(lambda i: links[0, i], shr(s16, 1) - 1))
    not_last = jnp.where((gx < NX - 1) | (gy < NY - 1), 1.0, 0.0).astype(F32)
    not_first = jnp.where((gx > 0) | (gy > 0), 1.0, 0.0).astype(F32)
    m1p = m1 * not_last
    m2p = m2 * not_last
    top = links[0, 7].astype(F32)

    def times(x, m):
        return (x.astype(F32) * m).astype(BF)

    def face_copy(ph, way, al):
        return pltpu.make_async_remote_copy(
            src_ref=stage.at[ph, way, al],
            dst_ref=ghost.at[ph, way, al],
            send_sem=hsend.at[ph, way, al],
            recv_sem=hrecv.at[ph, way, al],
            device_id=nxt if way else prv,
            device_id_type=MESH,
        )

    def end_copy(ph, way):
        return pltpu.make_async_remote_copy(
            src_ref=astage.at[ph, way],
            dst_ref=aghost.at[ph, way],
            send_sem=asend.at[ph, way],
            recv_sem=arecv.at[ph, way],
            device_id=nxt if way else prv,
            device_id_type=MESH,
        )

    def publish(ph, arr, al):
        stage[ph, 0, al, 0] = arr[al + 1, 1, 1:9]
        stage[ph, 0, al, 1] = arr[al + 1, 1:9, 1]
        stage[ph, 1, al, 0] = times(arr[al + 1, 8, 1:9], m1)
        stage[ph, 1, al, 1] = times(arr[al + 1, 1:9, 8], m2)
        face_copy(ph, 0, al).start()
        face_copy(ph, 1, al).start()

    def publish_end(ph, arr, way):
        for g in range(4):
            rows = arr[4 if way else 1, 1 + 2 * g : 3 + 2 * g, 1:9].reshape(256, 128)
            face = mm(pick[way], rows)
            if way:
                face = face * top
            astage[ph, way, g * 16 : g * 16 + 16] = face.astype(BF)
        end_copy(ph, way).start()

    def absorb(ph, arr, al):
        face_copy(ph, 0, al).wait_recv()
        face_copy(ph, 1, al).wait_recv()
        arr[al + 1, 9, 1:9] = times(ghost[ph, 0, al, 0], m1p)
        arr[al + 1, 1:9, 9] = times(ghost[ph, 0, al, 1], m2p)
        arr[al + 1, 0, 1:9] = times(ghost[ph, 1, al, 0], not_first)
        arr[al + 1, 1:9, 0] = times(ghost[ph, 1, al, 1], not_first)

    def absorb_ends(ph, arr):
        end_copy(ph, 0).wait_recv()
        end_copy(ph, 1).wait_recv()
        for g in range(4):
            bs = slice(1 + 2 * g, 3 + 2 * g)
            gs = slice(g * 16, g * 16 + 16)
            rows = mm(up1[...], arr[1, bs, 1:9].reshape(256, 128)).reshape(16, 16, 128) * ma
            end = mm(spread[1], aghost[ph, 0, gs]).reshape(16, 16, 128) * (top * not_last)
            arr[5, bs, 1:9] = (rows + end).astype(BF).reshape(2, 8, 16, 128)
            rows = mm(dn1[...], arr[4, bs, 1:9].reshape(256, 128)).reshape(16, 16, 128) * mb
            end = mm(spread[0], aghost[ph, 1, gs]).reshape(16, 16, 128) * not_first
            arr[0, bs, 1:9] = (rows + end).astype(BF).reshape(2, 8, 16, 128)

    def taps(arr, al, b0, nb):
        n = nb * 128
        win = [
            arr[al + 1, 1 + b0 : 1 + b0 + nb, 1:9],
            arr[al + 2, 1 + b0 : 1 + b0 + nb, 1:9],
            arr[al, 1 + b0 : 1 + b0 + nb, 1:9],
            arr[al + 1, 2 + b0 : 2 + b0 + nb, 1:9],
            arr[al + 1, b0 : b0 + nb, 1:9],
            arr[al + 1, 1 + b0 : 1 + b0 + nb, 2:10],
            arr[al + 1, 1 + b0 : 1 + b0 + nb, 0:8],
        ]
        return jnp.concatenate([w.reshape(n, 128) for w in win], axis=1)

    loads[0].wait()
    pl.semaphore_wait(barrier, 25)

    def send_ids(o, carry):
        pltpu.make_async_remote_copy(
            src_ref=ids,
            dst_ref=idl.at[gx],
            send_sem=isend,
            recv_sem=irecv,
            device_id=(gy, (gx + o) % NX),
            device_id_type=MESH,
        ).start()
        return carry

    def bring(t, carry):
        al = (t + 3) % 4
        for g in (0, 2):
            two = [
                xv[:, :, al, k * 16 : k * 16 + 16, :].reshape(256, 128) for k in (g, g + 1)
            ]
            moved = mm(perm[...], jnp.concatenate(two, axis=1)).astype(BF)
            for n in range(2):
                fa[al + 1, 1 + 2 * (g + n) : 3 + 2 * (g + n), 1:9] = moved[
                    :, n * 128 : n * 128 + 128
                ].reshape(2, 8, 16, 128)
        publish(0, fa, al)
        return carry

    astage[0, 0] = xv[0, 0, 0]
    astage[0, 1] = (xv[7, 1, 3].astype(F32) * top).astype(BF)
    end_copy(0, 0).start()
    end_copy(0, 1).start()
    lax.fori_loop(0, 4, bring, 0)
    idl[gx] = ids[...]

    loads[1].wait()
    absorb_ends(0, fa)

    def conv_one(t, carry):
        al = (t + 3) % 4
        absorb(0, fa, al)
        for b0 in (0, 4):
            h = mm(taps(fa, al, b0, 4), w1[...])
            fb[al + 1, 1 + b0 : 5 + b0, 1:9] = (
                jnp.maximum(h, 0.0).astype(BF).reshape(4, 8, 16, 128)
            )
        publish(1, fb, al)

        @pl.when(t == 0)
        def _():
            publish_end(1, fb, 1)

        @pl.when(t == 1)
        def _():
            publish_end(1, fb, 0)

        return carry

    lax.fori_loop(0, 4, conv_one, 0)
    lax.fori_loop(1, NX, send_ids, 0)

    lane = iota((1, 128), 1)
    slot_lane = jnp.zeros((1, 128), jnp.int32)
    for i in range(8):
        slot_lane = jnp.where((shr(lane, 1) & 7) == i, slot[i], slot_lane)
    k = iota((512, 128), 0)
    rho = iota((512, 128), 1)
    slot_mat = onehot(
        (shr(k, 4) == slot_lane) & ((shr(k, 1) & 7) == shr(rho, 4)) & ((k & 1) == (rho & 1))
    )
    row_block = shr(iota((128, 256), 0), 1) & 7
    row_level = jnp.zeros((128, 256), jnp.int32)
    for i in range(8):
        row_level = jnp.where(row_block == i, level[i], row_level)

    loads[2].wait()
    loads[3].wait()
    absorb_ends(1, fb)

    def column_copy(al, o):
        to = (gx + o) % NX
        return pltpu.make_async_remote_copy(
            src_ref=sbuf.at[al, to],
            dst_ref=rbuf.at[al, gx],
            send_sem=tsend.at[al],
            recv_sem=trecv.at[al],
            device_id=(gy, to),
            device_id_type=MESH,
        )

    def conv_two(t, carry):
        al = (t + 3) % 4
        absorb(1, fb, al)
        parts = []
        for b0 in (0, 4):
            v = mm(taps(fb, al, b0, 4), w2[...])
            v = v + fa[al + 1, 1 + b0 : 5 + b0, 1:9].reshape(512, 128).astype(F32)
            v = jnp.maximum(v, 0.0).astype(BF).reshape(4, 8, 16, 128)
            parts.append(
                jnp.concatenate([v[:, c].reshape(64, 128) for c in range(8)], axis=1)
            )
        rows = jnp.concatenate(parts, axis=0)
        lifted = jnp.zeros((128, 256), F32)
        for lv in range(4):
            lifted = jnp.where(row_level == lv, mm(rows, hw[lv]), lifted)
        high = lifted.astype(BF)
        low = (lifted - high.astype(F32)).astype(BF)
        sums = mm(slot_mat, high) + mm(slot_mat, low)
        sbuf[al] = sums.astype(BF).reshape(16, 32, 256)

        def send(o, c):
            column_copy(al, o).start()
            return c

        lax.fori_loop(1, NX, send, 0)
        rbuf[al, gx] = sbuf[al, gx]
        return carry

    lax.fori_loop(0, 4, conv_two, 0)

    pltpu.make_async_copy(idl.at[0:15], idl.at[0:15], irecv).wait()
    sel = onehot(iota((128, 512), 0) == 2 * gx + (shr(iota((128, 512), 1), 4) & 1))
    got = mm(idl[...].reshape(16, 128).astype(BF), sel)
    got = jnp.where(iota((16, 512), 0) == shr(iota((16, 512), 1), 5), got, 0.0)
    cid = jnp.sum(got, axis=0, keepdims=True)
    r = iota((512, 512), 0)
    k = iota((512, 512), 1)
    want = (shr(r, 1) & 7) * 4 + shr(r, 7)
    tile_mat = onehot(
        (cid == want.astype(F32)) & ((shr(r, 4) & 7) == (shr(k, 1) & 7)) & ((r & 1) == (k & 1))
    )

    def gather(t, carry):
        al = (t + 3) % 4
        pltpu.make_async_copy(rbuf.at[al, 0:15], rbuf.at[al, 0:15], trecv.at[al]).wait()
        tile = mm(tile_mat, rbuf[al].reshape(512, 256))
        bev[al + 2, 2:34] = tile.astype(BF).reshape(32, 16, 256)
        return carry

    lax.fori_loop(0, 4, gather, 0)

    cstage[0] = bev[2:6, 2:4]
    cstage[1] = bev[2:6, 32:34]
    for n in range(2):
        for g in range(2):
            xs = slice(2 + 16 * g, 18 + 16 * g)
            gs = slice(16 * g, 16 * g + 16)
            rstage[0, n, gs] = mm(pick[0], bev[2 + n, xs].reshape(256, 256)).astype(BF)
            rstage[1, n, gs] = mm(pick[1], bev[4 + n, xs].reshape(256, 256)).astype(BF)

    def rim(n, src, dst, where):
        return pltpu.make_async_remote_copy(
            src_ref=src,
            dst_ref=dst,
            send_sem=msend.at[n],
            recv_sem=mrecv.at[n],
            device_id=where,
            device_id_type=MESH,
        )

    rims = [
        rim(0, cstage.at[0], cland.at[0], (gy, west)),
        rim(1, cstage.at[1], cland.at[1], (gy, east)),
        rim(2, rstage.at[0], rland.at[0], (north, gx)),
        rim(3, rstage.at[1], rland.at[1], (south, gx)),
        rim(4, rstage.at[0, :, 0:16], kland.at[0], (north, west)),
        rim(5, rstage.at[0, :, 16:32], kland.at[1], (north, east)),
        rim(6, rstage.at[1, :, 0:16], kland.at[2], (south, west)),
        rim(7, rstage.at[1, :, 16:32], kland.at[3], (south, east)),
    ]
    for c in rims:
        c.start()
    has_n = jnp.where(gy > 0, 1.0, 0.0).astype(F32)
    has_s = jnp.where(gy < NY - 1, 1.0, 0.0).astype(F32)
    has_w = jnp.where(gx > 0, 1.0, 0.0).astype(F32)
    has_e = jnp.where(gx < NX - 1, 1.0, 0.0).astype(F32)

    def carry_over(mat, arr, dst, src, x0, n):
        rows = mm(mat[0 : 16 * n, 0 : 16 * n], arr[src, x0 : x0 + n].reshape(16 * n, 256))
        arr[dst, x0 : x0 + n] = rows.astype(BF).reshape(n, 16, 256)

    for x0 in (2, 18):
        carry_over(dn1, bev, 1, 5, x0, 16)
        carry_over(up1, bev, 6, 2, x0, 16)

    loads[4].wait()

    def plane_inner(yl, carry):
        win = [
            bev[yl + 1 + dy, 2 + dx : 32 + dx].reshape(480, 256)
            for dy in range(3)
            for dx in range(3)
        ]
        f = mm(jnp.concatenate(win, axis=1), p1[...])
        first[yl + 1, 2:32] = jnp.maximum(f, 0.0).astype(BF).reshape(30, 16, 256)
        return carry

    lax.fori_loop(0, 4, plane_inner, 0)
    for x0, n in ((2, 16), (18, 14)):
        carry_over(dn1, first, 0, 4, x0, n)
        carry_over(up1, first, 5, 1, x0, n)

    for c in rims:
        c.wait_recv()
    bev[2:6, 34:36] = times(cland[0], has_e)
    bev[2:6, 0:2] = times(cland[1], has_w)
    for x0 in (0, 34):
        carry_over(dn1, bev, 1, 5, x0, 2)
        carry_over(up1, bev, 6, 2, x0, 2)
    r = iota((32, 16), 0)
    q = iota((32, 16), 1)
    left_n, left_s = onehot(r == (q - 14) * 16), onehot(r == (q - 14) * 16 + 15)
    right_n, right_s = onehot(r == q * 16), onehot(r == q * 16 + 15)
    for n in range(2):
        at = 7 * n
        for g in range(2):
            xs = slice(2 + 16 * g, 18 + 16 * g)
            gs = slice(16 * g, 16 * g + 16)
            rows = mm(spread[0], rland[1, n, gs]) * has_n + mm(spread[1], rland[0, n, gs]) * has_s
            bev[at, xs] = rows.astype(BF).reshape(16, 16, 256)
        rows = mm(left_n, kland[3, n]) * (has_n * has_w) + mm(left_s, kland[1, n]) * (has_s * has_w)
        bev[at, 0:2] = rows.astype(BF).reshape(2, 16, 256)
        rows = mm(right_n, kland[2, n]) * (has_n * has_e) + mm(right_s, kland[0, n]) * (has_s * has_e)
        bev[at, 34:36] = rows.astype(BF).reshape(2, 16, 256)

    s8 = iota((36, 8, 256), 1)
    for dy in range(3):
        top0, top1 = ((0, 7), (7, 2), (2, 3))[dy]
        low0, low1 = ((4, 5), (5, 0), (0, 7))[dy]
        here = bev[top0][:, 0:8].astype(F32)
        after = pltpu.roll(bev[top1][:, 0:8].astype(F32), 1, 1)
        upper = jnp.where(s8 == 0, here, jnp.where(s8 == 1, after, 0.0))
        here = bev[low1][:, 8:16].astype(F32)
        before = pltpu.roll(bev[low0][:, 8:16].astype(F32), 7, 1)
        lower = jnp.where(s8 == 7, here, jnp.where(s8 == 6, before, 0.0))
        bev[8 + dy] = jnp.concatenate([upper, lower], axis=1).astype(BF)
    win = [bev[8 + dy, dx : dx + 34].reshape(544, 256) for dy in range(3) for dx in range(3)]
    f = mm(jnp.concatenate(win, axis=1), p1[...])
    edge[...] = jnp.maximum(f, 0.0).reshape(34, 16, 256)
    win = [
        jnp.concatenate(
            [
                bev[1 + dy : 5 + dy, x0 + dx : x0 + dx + 2].reshape(128, 256) for x0 in (0, 32)
            ],
            axis=0,
        )
        for dy in range(3)
        for dx in range(3)
    ]
    f = mm(jnp.concatenate(win, axis=1), p1[...])
    f = jnp.maximum(f, 0.0).reshape(2, 4, 2, 16, 256)
    first[1:5, 0:1] = (f[0, :, 0:1] * has_w).astype(BF)
    first[1:5, 1:2] = f[0, :, 1:2].astype(BF)
    first[1:5, 32:33] = f[1, :, 0:1].astype(BF)
    first[1:5, 33:34] = (f[1, :, 1:2] * has_e).astype(BF)
    edge[0:1] = edge[0:1] * has_w
    edge[33:34] = edge[33:34] * has_e
    for x0 in (0, 32):
        carry_over(dn1, first, 0, 4, x0, 2)
        carry_over(up1, first, 5, 1, x0, 2)
    s8 = iota((34, 8, 256), 1)
    upper = edge[:, 0:8]
    lower = edge[:, 8:16]

    def patch(slab, half, row, new):
        old = first[slab]
        keep = old[:, 0:8].astype(F32), old[:, 8:16].astype(F32)
        mixed = jnp.where(s8 == row, new, keep[half])
        both = [mixed, keep[1]] if half == 0 else [keep[0], mixed]
        first[slab] = jnp.concatenate(both, axis=1).astype(BF)

    patch(0, 0, 0, upper * has_n)
    patch(1, 0, 0, pltpu.roll(upper, 7, 1))
    patch(4, 1, 7, pltpu.roll(lower, 1, 1))
    patch(5, 1, 7, lower * has_s)
    base[...] = bev[2:6, 2:34]

    for ph in range(2):
        for way in range(2):
            end_copy(ph, way).wait_send()
            for al in range(4):
                face_copy(ph, way, al).wait_send()
    for al in range(4):
        pltpu.make_async_copy(sbuf.at[al, 0:15], sbuf.at[al, 0:15], tsend.at[al]).wait()
    pltpu.make_async_copy(idl.at[0:15], idl.at[0:15], isend).wait()
    for c in rims:
        c.wait_send()


def last_kernel(first, base, p2, out, buf, sems):
    r = iota((256, 256), 0)
    q = iota((256, 256), 1)
    perm = onehot(q == (r & 15) * 16 + shr(r, 4))
    copies = []
    for yl in range(4):
        win = [
            first[yl + dy, dx : dx + 32].reshape(512, 256) for dy in range(3) for dx in range(3)
        ]
        s = mm(jnp.concatenate(win, axis=1), p2[...])
        s = (s + base[yl].reshape(512, 256).astype(F32)).astype(BF)
        for g in range(2):
            moved = mm(perm, s[256 * g : 256 * g + 256]).astype(BF)
            buf[yl, :, 16 * g : 16 * g + 16, :] = moved.reshape(16, 16, 256)
        c = pltpu.make_async_copy(buf.at[yl], out.at[:, yl], sems.at[yl])
        c.start()
        copies.append(c)
    for c in copies:
        c.wait()


def local(
    features, links, block_slot, block_level, slot_column,
    conv_first, conv_second, height_w, plane_first, plane_second,
):
    hbm = pl.BlockSpec(memory_space=pltpu.HBM)
    vmem = pl.BlockSpec(memory_space=pltpu.VMEM)
    dma = pltpu.SemaphoreType.DMA
    operands = (
        features.reshape(8, 2, 4, 64, 128),
        links.T,
        block_slot,
        block_level,
        slot_column,
        conv_first.reshape(896, 128),
        conv_second.reshape(896, 128),
        height_w,
        plane_first.reshape(2304, 256),
    )
    first, base = pl.pallas_call(
        kernel,
        out_shape=[
            jax.ShapeDtypeStruct((6, 34, 16, 256), BF),
            jax.ShapeDtypeStruct((4, 32, 16, 256), BF),
        ],
        in_specs=[hbm] * 9,
        out_specs=[vmem, vmem],
        scratch_shapes=[
            pltpu.SMEM((3, 8), jnp.int32),
            pltpu.SMEM((8,), jnp.int32),
            pltpu.SMEM((8,), jnp.int32),
            pltpu.VMEM((1, 32), jnp.int32),
            pltpu.VMEM((8, 2, 4, 64, 128), BF),
            pltpu.VMEM((896, 128), BF),
            pltpu.VMEM((896, 128), BF),
            pltpu.VMEM((4, 1024, 256), BF),
            pltpu.VMEM((2304, 256), BF),
            pltpu.VMEM((6, 10, 10, 16, 128), BF),
            pltpu.VMEM((6, 10, 10, 16, 128), BF),
            pltpu.VMEM((2, 2, 4, 2, 8, 16, 128), BF),
            pltpu.VMEM((2, 2, 4, 2, 8, 16, 128), BF),
            pltpu.VMEM((2, 2, 64, 128), BF),
            pltpu.VMEM((2, 2, 64, 128), BF),
            pltpu.VMEM((256, 256), BF),
            pltpu.VMEM((256, 256), BF),
            pltpu.VMEM((256, 256), BF),
            pltpu.VMEM((2, 16, 256), BF),
            pltpu.VMEM((2, 256, 16), BF),
            pltpu.VMEM((4, 16, 32, 256), BF),
            pltpu.VMEM((4, 16, 32, 256), BF),
            pltpu.VMEM((1, 128), F32),
            pltpu.VMEM((16, 1, 128), F32),
            pltpu.VMEM((11, 36, 16, 256), BF),
            pltpu.VMEM((34, 16, 256), F32),
            pltpu.VMEM((2, 4, 2, 16, 256), BF),
            pltpu.VMEM((2, 4, 2, 16, 256), BF),
            pltpu.VMEM((2, 2, 32, 256), BF),
            pltpu.VMEM((2, 2, 32, 256), BF),
            pltpu.VMEM((4, 2, 16, 256), BF),
            dma((9,)),
            dma((2, 2, 4)),
            dma((2, 2, 4)),
            dma((2, 2)),
            dma((2, 2)),
            dma((4,)),
            dma((4,)),
            dma,
            dma,
            dma((8,)),
            dma((8,)),
        ],
        compiler_params=pltpu.CompilerParams(
            collective_id=0, has_side_effects=True, vmem_limit_bytes=40 * 2**20
        ),
    )(
        *[pltpu.with_memory_space_constraint(x, pltpu.HBM) for x in operands]
    )
    out = pl.pallas_call(
        last_kernel,
        out_shape=jax.ShapeDtypeStruct((16, 4, 32, 256), BF),
        in_specs=[vmem, vmem, vmem],
        out_specs=hbm,
        scratch_shapes=[pltpu.VMEM((4, 16, 32, 256), BF), dma((4,))],
        compiler_params=pltpu.CompilerParams(vmem_limit_bytes=24 * 2**20),
    )(first, base, plane_second.reshape(2304, 256))
    return out.reshape(64, 32, 256)


def solution(mesh):
    in_specs = (
        P(("gy", "gx"), None, None),
        P(("gy", "gx"), None),
        P(("gy", "gx")),
        P(("gy", "gx")),
        P(("gy", "gx"), None),
        P(),
        P(),
        P(),
        P(),
        P(),
    )
    return jax.shard_map(
        local, mesh=mesh, in_specs=in_specs, out_specs=P("gy", "gx", None), check_vma=False
    )
```

```python
import jax
import jax.numpy as jnp
from jax import lax
from jax.experimental import pallas as pl
from jax.experimental.pallas import tpu as pltpu
from jax.sharding import PartitionSpec as P

NY = 8
NX = 16
MESH = pl.DeviceIdType.MESH
F32 = jnp.float32
BF = jnp.bfloat16


def iota(shape, dim):
    return lax.broadcasted_iota(jnp.int32, shape, dim)


def shr(x, n):
    return lax.shift_right_logical(x, jnp.int32(n))


def onehot(cond):
    return jnp.where(cond, 1.0, 0.0).astype(BF)


def mm(a, b):
    return jnp.dot(a, b, preferred_element_type=F32)


def halves(x):
    x = x.astype(F32)
    return x[:, 0:8], x[:, 8:16]


def one_up(x, last, scale=(1.0, 1.0)):
    low, high = (pltpu.roll(h, 7, 1) for h in halves(x))
    end = iota(low.shape, 1) == 7
    low = jnp.where(end, high, low) * scale[0]
    high = jnp.where(end, last, high * scale[1])
    return jnp.concatenate([low, high], axis=1).astype(BF)


def one_down(x, head, scale=(1.0, 1.0)):
    low, high = (pltpu.roll(h, 1, 1) for h in halves(x))
    end = iota(low.shape, 1) == 0
    high = jnp.where(end, low, high) * scale[1]
    low = jnp.where(end, head, low * scale[0])
    return jnp.concatenate([low, high], axis=1).astype(BF)


def kernel(
    x_hbm, links_hbm, slot_hbm, level_hbm, ids_hbm, w1_hbm, w2_hbm, h_hbm, p1_hbm,
    first, base,
    links, slot, level, ids_in, xv, w1, w2, hw, p1,
    fa, fb, stage, ghost, astage, aghost,
    rows32, sbuf, rbuf, ids, idl,
    bev, edge, tile32, rim32, cstage, cland, rstage, rland, kland,
    wsem, hsend, hrecv, asend, arecv, tsend, trecv, isend, irecv, msend, mrecv,
):
    gy = lax.axis_index("gy")
    gx = lax.axis_index("gx")
    nxt = ((gy + (gx + 1) // NX) % NY, (gx + 1) % NX)
    prv = ((gy + NY - 1 + (gx + NX - 1) // NX) % NY, (gx + NX - 1) % NX)
    north, south = (gy + NY - 1) % NY, (gy + 1) % NY
    west, east = (gx + NX - 1) % NX, (gx + 1) % NX

    loads = [
        pltpu.make_async_copy(s, d, wsem.at[n])
        for n, (s, d) in enumerate(
            [
                (x_hbm, xv), (w1_hbm, w1), (w2_hbm, w2), (h_hbm, hw), (p1_hbm, p1),
                (links_hbm, links), (slot_hbm, slot), (level_hbm, level), (ids_hbm, ids_in),
            ]
        )
    ]
    for load in loads:
        load.start()

    barrier = pltpu.get_barrier_semaphore()

    def hello(where):
        pl.semaphore_signal(barrier, inc=1, device_id=where, device_id_type=MESH)

    has_nxt = (gx < NX - 1) | (gy < NY - 1)
    has_prv = (gx > 0) | (gy > 0)
    can_n, can_s, can_w, can_e = gy > 0, gy < NY - 1, gx > 0, gx < NX - 1
    no = jnp.logical_not

    def greet(o, carry):
        hello((gy, (gx + o) % NX))
        return carry

    greeted = jnp.int32(NX - 1)
    for there, where in (
        (has_nxt, nxt),
        (has_prv, prv),
        (can_n, (north, gx)),
        (can_s, (south, gx)),
        (can_n & can_w, (north, west)),
        (can_n & can_e, (north, east)),
        (can_s & can_w, (south, west)),
        (can_s & can_e, (south, east)),
    ):
        greeted = greeted + there.astype(jnp.int32)

        @pl.when(there)
        def _(where=where):
            hello(where)

    lax.fori_loop(1, NX, greet, 0)

    for there, land in (
        (has_nxt, (ghost.at[:, 0], aghost.at[:, 0])),
        (has_prv, (ghost.at[:, 1], aghost.at[:, 1])),
        (can_e, (cland.at[0],)),
        (can_w, (cland.at[1],)),
        (can_s, (rland.at[0],)),
        (can_n, (rland.at[1],)),
        (can_s & can_e, (kland.at[0],)),
        (can_s & can_w, (kland.at[1],)),
        (can_n & can_e, (kland.at[2],)),
        (can_n & can_w, (kland.at[3],)),
    ):

        @pl.when(no(there))
        def _(land=land):
            for ref in land:
                ref[...] = jnp.zeros(ref.shape, BF)

    for load in loads[5:]:
        load.wait()
    ids[...] = jnp.zeros((1, 128), F32)
    ids[0:1, 0:32] = ids_in[...].astype(F32)

    s16 = iota((16, 128), 0)

    def per_block(read, index):
        m = jnp.zeros((16, 128), F32)
        for i in range(8):
            m = jnp.where(index == i, read(i).astype(F32), m)
        return m

    m1 = per_block(lambda i: links[1, i], shr(s16, 1))
    m2 = per_block(lambda i: links[2, i], shr(s16, 1))
    ma = jnp.where((s16 & 1) == 0, 1.0, per_block(lambda i: links[0, i], shr(s16, 1)))
    mb = jnp.where((s16 & 1) == 1, 1.0, per_block(lambda i: links[0, i], shr(s16, 1) - 1))
    top = links[0, 7].astype(F32)

    def times(x, m):
        return (x.astype(F32) * m).astype(BF)

    def face_copy(ph, way, al):
        return pltpu.make_async_remote_copy(
            src_ref=stage.at[ph, way, al],
            dst_ref=ghost.at[ph, way, al],
            send_sem=hsend.at[ph, way, al],
            recv_sem=hrecv.at[ph, way, al],
            device_id=nxt if way else prv,
            device_id_type=MESH,
        )

    def end_copy(ph, way):
        return pltpu.make_async_remote_copy(
            src_ref=astage.at[ph, way],
            dst_ref=aghost.at[ph, way],
            send_sem=asend.at[ph, way],
            recv_sem=arecv.at[ph, way],
            device_id=nxt if way else prv,
            device_id_type=MESH,
        )

    def ring(do, way, back=False):
        pl.when(has_nxt if (way == 1) != back else has_prv)(do)

    def send_faces(ph, al):
        for way in range(2):
            ring(lambda way=way: face_copy(ph, way, al).start(), way)

    def faces_sent(ph, al):
        for way in range(2):
            ring(lambda way=way: face_copy(ph, way, al).wait_send(), way)

    def lay_out(ph, arr, al):
        stage[ph, 0, al, 0] = arr[al + 1, 1, 1:9]
        stage[ph, 0, al, 1] = arr[al + 1, 1:9, 1]
        stage[ph, 1, al, 0] = times(arr[al + 1, 8, 1:9], m1)
        stage[ph, 1, al, 1] = times(arr[al + 1, 1:9, 8], m2)

    def send_end(ph, way):
        ring(lambda: end_copy(ph, way).start(), way)

    def absorb(ph, arr, al):
        for way in range(2):
            ring(lambda way=way: face_copy(ph, way, al).wait_recv(), way, True)
        arr[al + 1, 9, 1:9] = times(ghost[ph, 0, al, 0], m1)
        arr[al + 1, 1:9, 9] = times(ghost[ph, 0, al, 1], m2)
        arr[al + 1, 0, 1:9] = ghost[ph, 1, al, 0]
        arr[al + 1, 1:9, 0] = ghost[ph, 1, al, 1]

    def absorb_ends(ph, arr):
        for way in range(2):
            ring(lambda way=way: end_copy(ph, way).wait_recv(), way, True)
        rows32[0, pl.ds(15, 64, stride=16), :] = aghost[ph, 0].astype(F32) * top
        rows32[0, pl.ds(0, 64, stride=16), :] = aghost[ph, 1].astype(F32)
        for b in range(8):
            low, high = halves(rows32[0, b * 128 : b * 128 + 128].reshape(8, 16, 128))
            arr[5, 1 + b, 1:9] = one_up(arr[1, 1 + b, 1:9], high, (ma[0:8], ma[8:16]))
            arr[0, 1 + b, 1:9] = one_down(arr[4, 1 + b, 1:9], low, (mb[0:8], mb[8:16]))

    def taps(arr, al, b0, nb):
        n = nb * 128
        win = [
            arr[al + 1, 1 + b0 : 1 + b0 + nb, 1:9],
            arr[al + 2, 1 + b0 : 1 + b0 + nb, 1:9],
            arr[al, 1 + b0 : 1 + b0 + nb, 1:9],
            arr[al + 1, 2 + b0 : 2 + b0 + nb, 1:9],
            arr[al + 1, b0 : b0 + nb, 1:9],
            arr[al + 1, 1 + b0 : 1 + b0 + nb, 2:10],
            arr[al + 1, 1 + b0 : 1 + b0 + nb, 0:8],
        ]
        return jnp.concatenate([w.reshape(n, 128) for w in win], axis=1)

    loads[0].wait()

    def send_ids(o, carry):
        pltpu.make_async_remote_copy(
            src_ref=ids,
            dst_ref=idl.at[gx],
            send_sem=isend,
            recv_sem=irecv,
            device_id=(gy, (gx + o) % NX),
            device_id_type=MESH,
        ).start()
        return carry

    astage[0, 0] = xv[0, 0, 0]
    astage[0, 1] = (xv[7, 1, 3].astype(F32) * top).astype(BF)
    for t in range(4):
        al = (t + 3) % 4
        rows32[t % 2] = xv[:, :, al].reshape(1024, 128).astype(F32)
        for b in range(8):
            for c in range(8):
                cell = rows32[t % 2, pl.ds(8 * b + c, 16, stride=64), :]
                fa[al + 1, 1 + b, 1 + c] = cell.astype(BF)
        lay_out(0, fa, al)
    idl[gx] = ids[...]
    pl.semaphore_wait(barrier, greeted)
    send_end(0, 0)
    send_end(0, 1)
    send_faces(0, 3)
    send_faces(0, 0)
    faces_sent(0, 3)
    send_faces(0, 1)
    faces_sent(0, 0)
    send_faces(0, 2)

    loads[1].wait()
    absorb_ends(0, fa)

    for t in range(4):
        al = (t + 3) % 4
        absorb(0, fa, al)
        for b0 in (0, 4):
            h = jnp.maximum(mm(taps(fa, al, b0, 4), w1[...]), 0.0)
            fb[al + 1, 1 + b0 : 5 + b0, 1:9] = h.astype(BF).reshape(4, 8, 16, 128)
            if t < 2:
                rows32[t, b0 * 128 : b0 * 128 + 512] = h
        if t == 0:
            astage[1, 1] = (rows32[0, pl.ds(15, 64, stride=16), :] * top).astype(BF)
            send_end(1, 1)
        if t == 1:
            astage[1, 0] = rows32[1, pl.ds(0, 64, stride=16), :].astype(BF)
            send_end(1, 0)
        lay_out(1, fb, al)
        send_faces(1, al)

    lax.fori_loop(1, NX, send_ids, 0)

    lane = iota((1, 128), 1)
    slot_lane = jnp.zeros((1, 128), jnp.int32)
    for i in range(8):
        slot_lane = jnp.where((shr(lane, 1) & 7) == i, slot[i], slot_lane)
    slot_lane = jnp.concatenate([slot_lane, slot_lane], axis=1)
    k = iota((512, 256), 0)
    rho = iota((512, 256), 1) & 127
    slot_mat = onehot(
        (shr(k, 4) == slot_lane) & ((shr(k, 1) & 7) == shr(rho, 4)) & ((k & 1) == (rho & 1))
    )
    row_block = shr(iota((128, 256), 0), 1) & 7
    row_level = jnp.zeros((128, 256), jnp.int32)
    for i in range(8):
        row_level = jnp.where(row_block == i, level[i], row_level)

    loads[2].wait()
    loads[3].wait()
    absorb_ends(1, fb)

    def column_copy(al, o):
        to = (gx + o) % NX
        return pltpu.make_async_remote_copy(
            src_ref=sbuf.at[al, to],
            dst_ref=rbuf.at[al, gx],
            send_sem=tsend.at[al],
            recv_sem=trecv.at[al],
            device_id=(gy, to),
            device_id_type=MESH,
        )

    for t in range(4):
        al = (t + 3) % 4
        absorb(1, fb, al)
        parts = []
        for b0 in (0, 4):
            v = mm(taps(fb, al, b0, 4), w2[...])
            v = v + fa[al + 1, 1 + b0 : 5 + b0, 1:9].reshape(512, 128).astype(F32)
            v = jnp.maximum(v, 0.0).astype(BF).reshape(4, 8, 16, 128)
            parts.append(
                jnp.concatenate([v[:, c].reshape(64, 128) for c in range(8)], axis=1)
            )
        rows = jnp.concatenate(parts, axis=0)
        lifted = jnp.zeros((128, 256), F32)
        for lv in range(4):
            lifted = jnp.where(row_level == lv, mm(rows, hw[lv]), lifted)
        high = lifted.astype(BF)
        low = (lifted - high.astype(F32)).astype(BF)
        sums = mm(slot_mat, jnp.concatenate([high, low], axis=0))
        sbuf[al] = sums.astype(BF).reshape(16, 32, 256)

        def send(o, c, al=al):
            column_copy(al, o).start()
            return c

        lax.fori_loop(1, NX, send, 0)
        rbuf[al, gx] = sbuf[al, gx]

    pltpu.make_async_copy(idl.at[0:15], idl.at[0:15], irecv).wait()
    sel = onehot(iota((128, 512), 0) == 2 * gx + (shr(iota((128, 512), 1), 4) & 1))
    got = mm(idl[...].reshape(16, 128).astype(BF), sel)
    got = jnp.where(iota((16, 512), 0) == shr(iota((16, 512), 1), 5), got, 0.0)
    cid = jnp.sum(got, axis=0, keepdims=True)
    r = iota((512, 512), 0)
    k = iota((512, 512), 1)
    want = (shr(r, 1) & 7) * 4 + shr(r, 7)
    tile_mat = onehot(
        (cid == want.astype(F32)) & ((shr(r, 4) & 7) == (shr(k, 1) & 7)) & ((r & 1) == (k & 1))
    )

    has_n = jnp.where(gy > 0, 1.0, 0.0).astype(F32)
    has_s = jnp.where(gy < NY - 1, 1.0, 0.0).astype(F32)
    has_w = jnp.where(gx > 0, 1.0, 0.0).astype(F32)
    has_e = jnp.where(gx < NX - 1, 1.0, 0.0).astype(F32)

    def rim(n, src, dst, where):
        return pltpu.make_async_remote_copy(
            src_ref=src,
            dst_ref=dst,
            send_sem=msend.at[n],
            recv_sem=mrecv.at[n],
            device_id=where,
            device_id_type=MESH,
        )

    early = [
        (can_w, can_e, rim(0, cstage.at[0, 0:3], cland.at[0, 0:3], (gy, west))),
        (can_e, can_w, rim(1, cstage.at[1, 0:3], cland.at[1, 0:3], (gy, east))),
        (can_n, can_s, rim(2, rstage.at[0], rland.at[0], (north, gx))),
        (can_n & can_w, can_s & can_e, rim(3, rstage.at[0, :, 0:16], kland.at[0], (north, west))),
        (can_n & can_e, can_s & can_w, rim(4, rstage.at[0, :, 16:32], kland.at[1], (north, east))),
    ]
    late = [
        (can_w, can_e, rim(5, cstage.at[0, 3:4], cland.at[0, 3:4], (gy, west))),
        (can_e, can_w, rim(6, cstage.at[1, 3:4], cland.at[1, 3:4], (gy, east))),
        (can_s, can_n, rim(7, rstage.at[1], rland.at[1], (south, gx))),
        (can_s & can_w, can_n & can_e, rim(8, rstage.at[1, :, 0:16], kland.at[2], (south, west))),
        (can_s & can_e, can_n & can_w, rim(9, rstage.at[1, :, 16:32], kland.at[3], (south, east))),
    ]
    rims = early + late

    def carry_down(arr, dst, src, x0, n):
        arr[dst, x0 : x0 + n] = one_down(arr[src, x0 : x0 + n], 0.0)

    def carry_up(arr, dst, src, x0, n):
        arr[dst, x0 : x0 + n] = one_up(arr[src, x0 : x0 + n], 0.0)

    def plane_inner(yl):
        win = [
            bev[yl + 1 + dy, 2 + dx : 32 + dx].reshape(480, 256)
            for dy in range(3)
            for dx in range(3)
        ]
        f = mm(jnp.concatenate(win, axis=1), p1[...])
        first[yl + 1, 2:32] = jnp.maximum(f, 0.0).astype(BF).reshape(30, 16, 256)

    for t in range(4):
        al = (t + 3) % 4
        pltpu.make_async_copy(rbuf.at[al, 0:15], rbuf.at[al, 0:15], trecv.at[al]).wait()
        tile = mm(tile_mat, rbuf[al].reshape(512, 256))
        bev[al + 2, 2:34] = tile.astype(BF).reshape(32, 16, 256)
        for c in range(2):
            cs = slice(128 * c, 128 * c + 128)
            tile32[c] = tile[:, cs]
            edge_rows = tile32[c, pl.ds(0 if al < 2 else 15, 32, stride=16), :]
            rstage[al // 2, al % 2, :, cs] = edge_rows.astype(BF)
        cstage[0, t] = bev[al + 2, 2:4]
        cstage[1, t] = bev[al + 2, 32:34]
        if t == 2:
            for to, back, c in early:
                pl.when(to)(c.start)
            loads[4].wait()
            carry_down(bev, 1, 5, 2, 32)
            plane_inner(0)
        if t == 3:
            for to, back, c in late:
                pl.when(to)(c.start)
            carry_up(bev, 6, 2, 2, 32)
            for yl in (3, 1, 2):
                plane_inner(yl)
            carry_down(first, 0, 4, 2, 30)
            carry_up(first, 5, 1, 2, 30)

    for to, back, c in rims:
        pl.when(back)(c.wait_recv)
    for t in range(4):
        al = (t + 3) % 4
        bev[al + 2, 34:36] = cland[0, t]
        bev[al + 2, 0:2] = cland[1, t]
    for x0 in (0, 34):
        carry_down(bev, 1, 5, x0, 2)
        carry_up(bev, 6, 2, x0, 2)
    for n in range(2):
        for c in range(2):
            cs = slice(128 * c, 128 * c + 128)
            for sub, way in ((0, 1), (15, 0)):
                rim32[n, c, pl.ds(32 + sub, 32, stride=16), :] = rland[way, n, :, cs].astype(F32)
                corner = kland[2 * way + 1, n, :, cs].astype(F32)[14:16]
                rim32[n, c, pl.ds(sub, 2, stride=16), :] = corner
                corner = kland[2 * way, n, :, cs].astype(F32)[0:2]
                rim32[n, c, pl.ds(544 + sub, 2, stride=16), :] = corner

    def map_half(slab, half):
        hs = slice(8 * half, 8 * half + 8)
        if slab in (0, 7):
            both = [rim32[slab // 7, c].reshape(36, 16, 128)[:, hs] for c in range(2)]
            return jnp.concatenate(both, axis=2)
        return bev[slab].astype(F32)[:, hs]

    s8 = iota((36, 8, 256), 1)
    for dy in range(3):
        top0, top1 = ((0, 7), (7, 2), (2, 3))[dy]
        low0, low1 = ((4, 5), (5, 0), (0, 7))[dy]
        here = map_half(top0, 0)
        after = pltpu.roll(map_half(top1, 0), 1, 1)
        upper = jnp.where(s8 == 0, here, jnp.where(s8 == 1, after, 0.0))
        here = map_half(low1, 1)
        before = pltpu.roll(map_half(low0, 1), 7, 1)
        lower = jnp.where(s8 == 7, here, jnp.where(s8 == 6, before, 0.0))
        bev[8 + dy] = jnp.concatenate([upper, lower], axis=1).astype(BF)
    win = [bev[8 + dy, dx : dx + 34].reshape(544, 256) for dy in range(3) for dx in range(3)]
    f = mm(jnp.concatenate(win, axis=1), p1[...])
    edge[...] = jnp.maximum(f, 0.0).reshape(34, 16, 256)
    win = [
        jnp.concatenate(
            [
                bev[1 + dy : 5 + dy, x0 + dx : x0 + dx + 2].reshape(128, 256) for x0 in (0, 32)
            ],
            axis=0,
        )
        for dy in range(3)
        for dx in range(3)
    ]
    f = mm(jnp.concatenate(win, axis=1), p1[...])
    f = jnp.maximum(f, 0.0).reshape(2, 4, 2, 16, 256)
    first[1:5, 0:1] = (f[0, :, 0:1] * has_w).astype(BF)
    first[1:5, 1:2] = f[0, :, 1:2].astype(BF)
    first[1:5, 32:33] = f[1, :, 0:1].astype(BF)
    first[1:5, 33:34] = (f[1, :, 1:2] * has_e).astype(BF)
    edge[0:1] = edge[0:1] * has_w
    edge[33:34] = edge[33:34] * has_e
    for x0 in (0, 32):
        carry_down(first, 0, 4, x0, 2)
        carry_up(first, 5, 1, x0, 2)
    s8 = iota((34, 8, 256), 1)
    upper = edge[:, 0:8]
    lower = edge[:, 8:16]

    def patch(slab, half, row, new):
        old = first[slab]
        keep = old[:, 0:8].astype(F32), old[:, 8:16].astype(F32)
        mixed = jnp.where(s8 == row, new, keep[half])
        both = [mixed, keep[1]] if half == 0 else [keep[0], mixed]
        first[slab] = jnp.concatenate(both, axis=1).astype(BF)

    patch(0, 0, 0, upper * has_n)
    patch(1, 0, 0, pltpu.roll(upper, 7, 1))
    patch(4, 1, 7, pltpu.roll(lower, 1, 1))
    patch(5, 1, 7, lower * has_s)
    base[...] = bev[2:6, 2:34]

    for ph in range(2):
        for way in range(2):
            ring(lambda ph=ph, way=way: end_copy(ph, way).wait_send(), way)
        for al in range(4):
            if ph == 1 or al in (1, 2):
                faces_sent(ph, al)
    for al in range(4):
        pltpu.make_async_copy(sbuf.at[al, 0:15], sbuf.at[al, 0:15], tsend.at[al]).wait()
    pltpu.make_async_copy(idl.at[0:15], idl.at[0:15], isend).wait()
    for to, back, c in rims:
        pl.when(to)(c.wait_send)


def last_kernel(first, base, p2, out, rows32, buf, sems):
    copies = []
    for yl in range(4):
        win = [
            first[yl + dy, dx : dx + 32].reshape(512, 256) for dy in range(3) for dx in range(3)
        ]
        s = mm(jnp.concatenate(win, axis=1), p2[...])
        s = s + base[yl].reshape(512, 256).astype(F32)
        for c in range(2):
            cs = slice(128 * c, 128 * c + 128)
            rows32[yl % 2, c] = s[:, cs]
            for y in range(16):
                buf[yl, y, :, cs] = rows32[yl % 2, c, pl.ds(y, 32, stride=16), :].astype(BF)
        c = pltpu.make_async_copy(buf.at[yl], out.at[:, yl], sems.at[yl])
        c.start()
        copies.append(c)
    for c in copies:
        c.wait()


def local(
    features, links, block_slot, block_level, slot_column,
    conv_first, conv_second, height_w, plane_first, plane_second,
):
    hbm = pl.BlockSpec(memory_space=pltpu.HBM)
    vmem = pl.BlockSpec(memory_space=pltpu.VMEM)
    dma = pltpu.SemaphoreType.DMA
    operands = (
        features.reshape(8, 2, 4, 64, 128),
        links.T,
        block_slot,
        block_level,
        slot_column,
        conv_first.reshape(896, 128),
        conv_second.reshape(896, 128),
        height_w,
        plane_first.reshape(2304, 256),
    )
    first, base = pl.pallas_call(
        kernel,
        out_shape=[
            jax.ShapeDtypeStruct((6, 34, 16, 256), BF),
            jax.ShapeDtypeStruct((4, 32, 16, 256), BF),
        ],
        in_specs=[hbm] * 9,
        out_specs=[vmem, vmem],
        scratch_shapes=[
            pltpu.SMEM((3, 8), jnp.int32),
            pltpu.SMEM((8,), jnp.int32),
            pltpu.SMEM((8,), jnp.int32),
            pltpu.VMEM((1, 32), jnp.int32),
            pltpu.VMEM((8, 2, 4, 64, 128), BF),
            pltpu.VMEM((896, 128), BF),
            pltpu.VMEM((896, 128), BF),
            pltpu.VMEM((4, 1024, 256), BF),
            pltpu.VMEM((2304, 256), BF),
            pltpu.VMEM((6, 10, 10, 16, 128), BF),
            pltpu.VMEM((6, 10, 10, 16, 128), BF),
            pltpu.VMEM((2, 2, 4, 2, 8, 16, 128), BF),
            pltpu.VMEM((2, 2, 4, 2, 8, 16, 128), BF),
            pltpu.VMEM((2, 2, 64, 128), BF),
            pltpu.VMEM((2, 2, 64, 128), BF),
            pltpu.VMEM((2, 1024, 128), F32),
            pltpu.VMEM((4, 16, 32, 256), BF),
            pltpu.VMEM((4, 16, 32, 256), BF),
            pltpu.VMEM((1, 128), F32),
            pltpu.VMEM((16, 1, 128), F32),
            pltpu.VMEM((11, 36, 16, 256), BF),
            pltpu.VMEM((34, 16, 256), F32),
            pltpu.VMEM((2, 512, 128), F32),
            pltpu.VMEM((2, 2, 576, 128), F32),
            pltpu.VMEM((2, 4, 2, 16, 256), BF),
            pltpu.VMEM((2, 4, 2, 16, 256), BF),
            pltpu.VMEM((2, 2, 32, 256), BF),
            pltpu.VMEM((2, 2, 32, 256), BF),
            pltpu.VMEM((4, 2, 16, 256), BF),
            dma((9,)),
            dma((2, 2, 4)),
            dma((2, 2, 4)),
            dma((2, 2)),
            dma((2, 2)),
            dma((4,)),
            dma((4,)),
            dma,
            dma,
            dma((10,)),
            dma((10,)),
        ],
        compiler_params=pltpu.CompilerParams(
            collective_id=0, has_side_effects=True, vmem_limit_bytes=40 * 2**20
        ),
    )(
        *[pltpu.with_memory_space_constraint(x, pltpu.HBM) for x in operands]
    )
    out = pl.pallas_call(
        last_kernel,
        out_shape=jax.ShapeDtypeStruct((16, 4, 32, 256), BF),
        in_specs=[vmem, vmem, vmem],
        out_specs=hbm,
        scratch_shapes=[
            pltpu.VMEM((2, 2, 512, 128), F32),
            pltpu.VMEM((4, 16, 32, 256), BF),
            dma((4,)),
        ],
        compiler_params=pltpu.CompilerParams(vmem_limit_bytes=24 * 2**20),
    )(first, base, plane_second.reshape(2304, 256))
    return out.reshape(64, 32, 256)


def solution(mesh):
    in_specs = (
        P(("gy", "gx"), None, None),
        P(("gy", "gx"), None),
        P(("gy", "gx")),
        P(("gy", "gx")),
        P(("gy", "gx"), None),
        P(),
        P(),
        P(),
        P(),
        P(),
    )
    return jax.shard_map(
        local, mesh=mesh, in_specs=in_specs, out_specs=P("gy", "gx", None), check_vma=False
    )
```

```python
import jax
import jax.numpy as jnp
from jax import lax
from jax.experimental import pallas as pl
from jax.experimental.pallas import tpu as pltpu
from jax.sharding import PartitionSpec as P

NY = 8
NX = 16
MESH = pl.DeviceIdType.MESH
F32 = jnp.float32
BF = jnp.bfloat16


def iota(shape, dim):
    return lax.broadcasted_iota(jnp.int32, shape, dim)


def shr(x, n):
    return lax.shift_right_logical(x, jnp.int32(n))


def onehot(cond):
    return jnp.where(cond, 1.0, 0.0).astype(BF)


def mm(a, b):
    return jnp.dot(a, b, preferred_element_type=F32)


def halves(x):
    x = x.astype(F32)
    return x[:, 0:8], x[:, 8:16]


def one_up(x, last, scale=(1.0, 1.0)):
    low, high = (pltpu.roll(h, 7, 1) for h in halves(x))
    end = iota(low.shape, 1) == 7
    low = jnp.where(end, high, low) * scale[0]
    high = jnp.where(end, last, high * scale[1])
    return jnp.concatenate([low, high], axis=1).astype(BF)


def one_down(x, head, scale=(1.0, 1.0)):
    low, high = (pltpu.roll(h, 1, 1) for h in halves(x))
    end = iota(low.shape, 1) == 0
    high = jnp.where(end, low, high) * scale[1]
    low = jnp.where(end, head, low * scale[0])
    return jnp.concatenate([low, high], axis=1).astype(BF)


def kernel(
    x_hbm, links_hbm, slot_hbm, level_hbm, ids_hbm, w1_hbm, w2_hbm, h_hbm, p1_hbm,
    first, base,
    links, slot, level, ids_in, xv, w1, w2, hw, p1,
    fa, fb, stage, ghost, astage, aghost,
    rows32, sbuf, rbuf, ids, idl,
    bev, edge, win32, tile32, rim32, cstage, cland, rstage, rland, kland,
    wsem, hsend, hrecv, asend, arecv, tsend, trecv, isend, irecv, msend, mrecv,
):
    gy = lax.axis_index("gy")
    gx = lax.axis_index("gx")
    nxt = ((gy + (gx + 1) // NX) % NY, (gx + 1) % NX)
    prv = ((gy + NY - 1 + (gx + NX - 1) // NX) % NY, (gx + NX - 1) % NX)
    north, south = (gy + NY - 1) % NY, (gy + 1) % NY
    west, east = (gx + NX - 1) % NX, (gx + 1) % NX

    loads = [
        pltpu.make_async_copy(s, d, wsem.at[n])
        for n, (s, d) in enumerate(
            [
                *[(x_hbm.at[:, :, al], xv.at[:, :, al]) for al in (3, 0, 1, 2)],
                (w1_hbm, w1), (w2_hbm, w2), (h_hbm, hw), (p1_hbm, p1),
                (links_hbm, links), (slot_hbm, slot), (level_hbm, level), (ids_hbm, ids_in),
            ]
        )
    ]
    for load in loads:
        load.start()

    barrier = pltpu.get_barrier_semaphore()

    def hello(where):
        pl.semaphore_signal(barrier, inc=1, device_id=where, device_id_type=MESH)

    has_nxt = (gx < NX - 1) | (gy < NY - 1)
    has_prv = (gx > 0) | (gy > 0)
    can_n, can_s, can_w, can_e = gy > 0, gy < NY - 1, gx > 0, gx < NX - 1
    no = jnp.logical_not

    def greet(o, carry):
        hello((gy, (gx + o) % NX))
        return carry

    greeted = jnp.int32(NX - 1)
    for there, where in (
        (has_nxt, nxt),
        (has_prv, prv),
        (can_n, (north, gx)),
        (can_s, (south, gx)),
        (can_n & can_w, (north, west)),
        (can_n & can_e, (north, east)),
        (can_s & can_w, (south, west)),
        (can_s & can_e, (south, east)),
    ):
        greeted = greeted + there.astype(jnp.int32)

        @pl.when(there)
        def _(where=where):
            hello(where)

    lax.fori_loop(1, NX, greet, 0)

    for there, land in (
        (has_nxt, (ghost.at[:, 0], aghost.at[:, 0])),
        (has_prv, (ghost.at[:, 1], aghost.at[:, 1])),
        (can_e, (cland.at[0],)),
        (can_w, (cland.at[1],)),
        (can_s, (rland.at[0],)),
        (can_n, (rland.at[1],)),
        (can_s & can_e, (kland.at[0],)),
        (can_s & can_w, (kland.at[1],)),
        (can_n & can_e, (kland.at[2],)),
        (can_n & can_w, (kland.at[3],)),
    ):

        @pl.when(no(there))
        def _(land=land):
            for ref in land:
                ref[...] = jnp.zeros(ref.shape, BF)

    for load in loads[8:]:
        load.wait()
    ids[...] = jnp.zeros((1, 128), F32)
    ids[0:1, 0:32] = ids_in[...].astype(F32)

    s16 = iota((16, 128), 0)

    def per_block(read, index):
        m = jnp.zeros((16, 128), F32)
        for i in range(8):
            m = jnp.where(index == i, read(i).astype(F32), m)
        return m

    m1 = per_block(lambda i: links[1, i], shr(s16, 1))
    m2 = per_block(lambda i: links[2, i], shr(s16, 1))
    ma = jnp.where((s16 & 1) == 0, 1.0, per_block(lambda i: links[0, i], shr(s16, 1)))
    mb = jnp.where((s16 & 1) == 1, 1.0, per_block(lambda i: links[0, i], shr(s16, 1) - 1))
    top = links[0, 7].astype(F32)

    def times(x, m):
        return (x.astype(F32) * m).astype(BF)

    def face_copy(ph, way, al):
        return pltpu.make_async_remote_copy(
            src_ref=stage.at[ph, way, al],
            dst_ref=ghost.at[ph, way, al],
            send_sem=hsend.at[ph, way, al],
            recv_sem=hrecv.at[ph, way, al],
            device_id=nxt if way else prv,
            device_id_type=MESH,
        )

    def end_copy(ph, way):
        return pltpu.make_async_remote_copy(
            src_ref=astage.at[ph, way],
            dst_ref=aghost.at[ph, way],
            send_sem=asend.at[ph, way],
            recv_sem=arecv.at[ph, way],
            device_id=nxt if way else prv,
            device_id_type=MESH,
        )

    def ring(do, way, back=False):
        pl.when(has_nxt if (way == 1) != back else has_prv)(do)

    def send_faces(ph, al):
        for way in range(2):
            ring(lambda way=way: face_copy(ph, way, al).start(), way)

    def faces_sent(ph, al):
        for way in range(2):
            ring(lambda way=way: face_copy(ph, way, al).wait_send(), way)

    def lay_out(ph, arr, al):
        stage[ph, 0, al, 0] = arr[al + 1, 1, 1:9]
        stage[ph, 0, al, 1] = arr[al + 1, 1:9, 1]
        stage[ph, 1, al, 0] = times(arr[al + 1, 8, 1:9], m1)
        stage[ph, 1, al, 1] = times(arr[al + 1, 1:9, 8], m2)

    def send_end(ph, way):
        ring(lambda: end_copy(ph, way).start(), way)

    def absorb(ph, arr, al):
        for way in range(2):
            ring(lambda way=way: face_copy(ph, way, al).wait_recv(), way, True)
        arr[al + 1, 9, 1:9] = times(ghost[ph, 0, al, 0], m1)
        arr[al + 1, 1:9, 9] = times(ghost[ph, 0, al, 1], m2)
        arr[al + 1, 0, 1:9] = ghost[ph, 1, al, 0]
        arr[al + 1, 1:9, 0] = ghost[ph, 1, al, 1]

    def absorb_ends(ph, arr):
        for way in range(2):
            ring(lambda way=way: end_copy(ph, way).wait_recv(), way, True)
        rows32[0, pl.ds(15, 64, stride=16), :] = aghost[ph, 0].astype(F32) * top
        rows32[0, pl.ds(0, 64, stride=16), :] = aghost[ph, 1].astype(F32)
        for b in range(8):
            low, high = halves(rows32[0, b * 128 : b * 128 + 128].reshape(8, 16, 128))
            arr[5, 1 + b, 1:9] = one_up(arr[1, 1 + b, 1:9], high, (ma[0:8], ma[8:16]))
            arr[0, 1 + b, 1:9] = one_down(arr[4, 1 + b, 1:9], low, (mb[0:8], mb[8:16]))

    def taps(arr, al, b0, nb):
        n = nb * 128
        win = [
            arr[al + 1, 1 + b0 : 1 + b0 + nb, 1:9],
            arr[al + 2, 1 + b0 : 1 + b0 + nb, 1:9],
            arr[al, 1 + b0 : 1 + b0 + nb, 1:9],
            arr[al + 1, 2 + b0 : 2 + b0 + nb, 1:9],
            arr[al + 1, b0 : b0 + nb, 1:9],
            arr[al + 1, 1 + b0 : 1 + b0 + nb, 2:10],
            arr[al + 1, 1 + b0 : 1 + b0 + nb, 0:8],
        ]
        return jnp.concatenate([w.reshape(n, 128) for w in win], axis=1)


    def send_ids(o, carry):
        pltpu.make_async_remote_copy(
            src_ref=ids,
            dst_ref=idl.at[gx],
            send_sem=isend,
            recv_sem=irecv,
            device_id=(gy, (gx + o) % NX),
            device_id_type=MESH,
        ).start()
        return carry

    def bring(t):
        al = (t + 3) % 4
        loads[t].wait()
        rows32[t % 2] = xv[:, :, al].reshape(1024, 128).astype(F32)
        for b in range(8):
            for c in range(8):
                cell = rows32[t % 2, pl.ds(8 * b + c, 16, stride=64), :]
                fa[al + 1, 1 + b, 1 + c] = cell.astype(BF)
        lay_out(0, fa, al)

    bring(0)
    astage[0, 1] = (xv[7, 1, 3].astype(F32) * top).astype(BF)
    bring(1)
    astage[0, 0] = xv[0, 0, 0]
    pl.semaphore_wait(barrier, greeted)
    send_end(0, 0)
    send_end(0, 1)
    send_faces(0, 3)
    send_faces(0, 0)
    bring(2)
    bring(3)
    idl[gx] = ids[...]
    faces_sent(0, 3)
    send_faces(0, 1)
    faces_sent(0, 0)
    send_faces(0, 2)

    loads[4].wait()
    absorb_ends(0, fa)

    for t in range(4):
        al = (t + 3) % 4
        absorb(0, fa, al)
        for b0 in (0, 4):
            h = jnp.maximum(mm(taps(fa, al, b0, 4), w1[...]), 0.0)
            fb[al + 1, 1 + b0 : 5 + b0, 1:9] = h.astype(BF).reshape(4, 8, 16, 128)
            if t < 2:
                rows32[t, b0 * 128 : b0 * 128 + 512] = h
        if t == 0:
            astage[1, 1] = (rows32[0, pl.ds(15, 64, stride=16), :] * top).astype(BF)
            send_end(1, 1)
        if t == 1:
            astage[1, 0] = rows32[1, pl.ds(0, 64, stride=16), :].astype(BF)
            send_end(1, 0)
        lay_out(1, fb, al)
        send_faces(1, al)

    lax.fori_loop(1, NX, send_ids, 0)

    lane = iota((1, 128), 1)
    slot_lane = jnp.zeros((1, 128), jnp.int32)
    for i in range(8):
        slot_lane = jnp.where((shr(lane, 1) & 7) == i, slot[i], slot_lane)
    slot_lane = jnp.concatenate([slot_lane, slot_lane], axis=1)
    k = iota((512, 256), 0)
    rho = iota((512, 256), 1) & 127
    slot_mat = onehot(
        (shr(k, 4) == slot_lane) & ((shr(k, 1) & 7) == shr(rho, 4)) & ((k & 1) == (rho & 1))
    )
    row_block = shr(iota((128, 256), 0), 1) & 7
    row_level = jnp.zeros((128, 256), jnp.int32)
    for i in range(8):
        row_level = jnp.where(row_block == i, level[i], row_level)

    loads[5].wait()
    loads[6].wait()
    absorb_ends(1, fb)

    def column_copy(al, o):
        to = (gx + o) % NX
        return pltpu.make_async_remote_copy(
            src_ref=sbuf.at[al, to],
            dst_ref=rbuf.at[al, gx],
            send_sem=tsend.at[al],
            recv_sem=trecv.at[al],
            device_id=(gy, to),
            device_id_type=MESH,
        )

    for t in range(4):
        al = (t + 3) % 4
        absorb(1, fb, al)
        parts = []
        for b0 in (0, 4):
            v = mm(taps(fb, al, b0, 4), w2[...])
            v = v + fa[al + 1, 1 + b0 : 5 + b0, 1:9].reshape(512, 128).astype(F32)
            v = jnp.maximum(v, 0.0).astype(BF).reshape(4, 8, 16, 128)
            parts.append(
                jnp.concatenate([v[:, c].reshape(64, 128) for c in range(8)], axis=1)
            )
        rows = jnp.concatenate(parts, axis=0)
        lifted = jnp.zeros((128, 256), F32)
        for lv in range(4):
            lifted = jnp.where(row_level == lv, mm(rows, hw[lv]), lifted)
        high = lifted.astype(BF)
        low = (lifted - high.astype(F32)).astype(BF)
        sums = mm(slot_mat, jnp.concatenate([high, low], axis=0))
        sbuf[al] = sums.astype(BF).reshape(16, 32, 256)

        def send(o, c, al=al):
            column_copy(al, o).start()
            return c

        lax.fori_loop(1, NX, send, 0)
        rbuf[al, gx] = sbuf[al, gx]

    pltpu.make_async_copy(idl.at[0:15], idl.at[0:15], irecv).wait()
    sel = onehot(iota((128, 512), 0) == 2 * gx + (shr(iota((128, 512), 1), 4) & 1))
    got = mm(idl[...].reshape(16, 128).astype(BF), sel)
    got = jnp.where(iota((16, 512), 0) == shr(iota((16, 512), 1), 5), got, 0.0)
    cid = jnp.sum(got, axis=0, keepdims=True)
    r = iota((512, 512), 0)
    k = iota((512, 512), 1)
    want = (shr(r, 1) & 7) * 4 + shr(r, 7)
    tile_mat = onehot(
        (cid == want.astype(F32)) & ((shr(r, 4) & 7) == (shr(k, 1) & 7)) & ((r & 1) == (k & 1))
    )

    has_n = jnp.where(gy > 0, 1.0, 0.0).astype(F32)
    has_s = jnp.where(gy < NY - 1, 1.0, 0.0).astype(F32)
    has_w = jnp.where(gx > 0, 1.0, 0.0).astype(F32)
    has_e = jnp.where(gx < NX - 1, 1.0, 0.0).astype(F32)

    def rim(n, src, dst, where):
        return pltpu.make_async_remote_copy(
            src_ref=src,
            dst_ref=dst,
            send_sem=msend.at[n],
            recv_sem=mrecv.at[n],
            device_id=where,
            device_id_type=MESH,
        )

    early = [
        (can_w, can_e, rim(0, cstage.at[0, 0:3], cland.at[0, 0:3], (gy, west))),
        (can_e, can_w, rim(1, cstage.at[1, 0:3], cland.at[1, 0:3], (gy, east))),
        (can_n, can_s, rim(2, rstage.at[0], rland.at[0], (north, gx))),
        (can_n & can_w, can_s & can_e, rim(3, rstage.at[0, :, 0:16], kland.at[0], (north, west))),
        (can_n & can_e, can_s & can_w, rim(4, rstage.at[0, :, 16:32], kland.at[1], (north, east))),
    ]
    late = [
        (can_w, can_e, rim(5, cstage.at[0, 3:4], cland.at[0, 3:4], (gy, west))),
        (can_e, can_w, rim(6, cstage.at[1, 3:4], cland.at[1, 3:4], (gy, east))),
        (can_s, can_n, rim(7, rstage.at[1], rland.at[1], (south, gx))),
        (can_s & can_w, can_n & can_e, rim(8, rstage.at[1, :, 0:16], kland.at[2], (south, west))),
        (can_s & can_e, can_n & can_w, rim(9, rstage.at[1, :, 16:32], kland.at[3], (south, east))),
    ]
    rims = early + late

    def carry_down(arr, dst, src, x0, n):
        arr[dst, x0 : x0 + n] = one_down(arr[src, x0 : x0 + n], 0.0)

    def carry_up(arr, dst, src, x0, n):
        arr[dst, x0 : x0 + n] = one_up(arr[src, x0 : x0 + n], 0.0)

    def plane_inner(yl):
        win = [
            bev[yl + 1 + dy, 2 + dx : 32 + dx].reshape(480, 256)
            for dy in range(3)
            for dx in range(3)
        ]
        f = mm(jnp.concatenate(win, axis=1), p1[...])
        first[yl + 1, 2:32] = jnp.maximum(f, 0.0).astype(BF).reshape(30, 16, 256)

    for t in range(4):
        al = (t + 3) % 4
        pltpu.make_async_copy(rbuf.at[al, 0:15], rbuf.at[al, 0:15], trecv.at[al]).wait()
        tile = mm(tile_mat, rbuf[al].reshape(512, 256))
        bev[al + 2, 2:34] = tile.astype(BF).reshape(32, 16, 256)
        for c in range(2):
            cs = slice(128 * c, 128 * c + 128)
            tile32[c] = tile[:, cs]
            edge_rows = tile32[c, pl.ds(0 if al < 2 else 15, 32, stride=16), :]
            rstage[al // 2, al % 2, :, cs] = edge_rows.astype(BF)
        cstage[0, t] = bev[al + 2, 2:4]
        cstage[1, t] = bev[al + 2, 32:34]
        if t == 2:
            for to, back, c in early:
                pl.when(to)(c.start)
            loads[7].wait()
            carry_down(bev, 1, 5, 2, 32)
            plane_inner(0)
        if t == 3:
            for to, back, c in late:
                pl.when(to)(c.start)
            carry_up(bev, 6, 2, 2, 32)
            for yl in (3, 1, 2):
                plane_inner(yl)
            carry_down(first, 0, 4, 2, 30)
            carry_up(first, 5, 1, 2, 30)

    for to, back, c in rims:
        pl.when(back)(c.wait_recv)
    for t in range(4):
        al = (t + 3) % 4
        bev[al + 2, 34:36] = cland[0, t]
        bev[al + 2, 0:2] = cland[1, t]
    for x0 in (0, 34):
        carry_down(bev, 1, 5, x0, 2)
        carry_up(bev, 6, 2, x0, 2)
    for n in range(2):
        for c in range(2):
            cs = slice(128 * c, 128 * c + 128)
            for sub, way in ((0, 1), (15, 0)):
                rim32[n, c, pl.ds(32 + sub, 32, stride=16), :] = rland[way, n, :, cs].astype(F32)
                corner = kland[2 * way + 1, n, :, cs].astype(F32)[14:16]
                rim32[n, c, pl.ds(sub, 2, stride=16), :] = corner
                corner = kland[2 * way, n, :, cs].astype(F32)[0:2]
                rim32[n, c, pl.ds(544 + sub, 2, stride=16), :] = corner

    def map_half(slab, half):
        hs = slice(8 * half, 8 * half + 8)
        if slab in (0, 7):
            both = [rim32[slab // 7, c].reshape(36, 16, 128)[:, hs] for c in range(2)]
            return jnp.concatenate(both, axis=2)
        return bev[slab].astype(F32)[:, hs]

    s8 = iota((36, 8, 256), 1)
    for dy in range(3):
        top0, top1 = ((0, 7), (7, 2), (2, 3))[dy]
        low0, low1 = ((4, 5), (5, 0), (0, 7))[dy]
        upper = jnp.where(s8 == 0, map_half(top0, 0), pltpu.roll(map_half(top1, 0), 1, 1))
        lower = jnp.where(s8 == 7, map_half(low1, 1), pltpu.roll(map_half(low0, 1), 7, 1))
        win32[dy] = jnp.where(s8 < 2, upper, jnp.where(s8 > 5, lower, 0.0))
    win = [
        win32[dy, dx : dx + 34].reshape(272, 256).astype(BF) for dy in range(3) for dx in range(3)
    ]
    f = mm(jnp.concatenate(win, axis=1), p1[...])
    edge[...] = jnp.maximum(f, 0.0).reshape(34, 8, 256)
    win = [
        jnp.concatenate(
            [
                bev[1 + dy : 5 + dy, x0 + dx : x0 + dx + 2].reshape(128, 256) for x0 in (0, 32)
            ],
            axis=0,
        )
        for dy in range(3)
        for dx in range(3)
    ]
    f = mm(jnp.concatenate(win, axis=1), p1[...])
    f = jnp.maximum(f, 0.0).reshape(2, 4, 2, 16, 256)
    first[1:5, 0:1] = (f[0, :, 0:1] * has_w).astype(BF)
    first[1:5, 1:2] = f[0, :, 1:2].astype(BF)
    first[1:5, 32:33] = f[1, :, 0:1].astype(BF)
    first[1:5, 33:34] = (f[1, :, 1:2] * has_e).astype(BF)
    edge[0:1] = edge[0:1] * has_w
    edge[33:34] = edge[33:34] * has_e
    for x0 in (0, 32):
        carry_down(first, 0, 4, x0, 2)
        carry_up(first, 5, 1, x0, 2)
    s8 = iota((34, 8, 256), 1)
    rows = edge[...]

    def patch(slab, half, row, new):
        old = first[slab]
        keep = old[:, 0:8].astype(F32), old[:, 8:16].astype(F32)
        mixed = jnp.where(s8 == row, new, keep[half])
        both = [mixed, keep[1]] if half == 0 else [keep[0], mixed]
        first[slab] = jnp.concatenate(both, axis=1).astype(BF)

    patch(0, 0, 0, rows * has_n)
    patch(1, 0, 0, pltpu.roll(rows, 7, 1))
    patch(4, 1, 7, pltpu.roll(rows, 1, 1))
    patch(5, 1, 7, rows * has_s)
    base[...] = bev[2:6, 2:34]

    for ph in range(2):
        for way in range(2):
            ring(lambda ph=ph, way=way: end_copy(ph, way).wait_send(), way)
        for al in range(4):
            if ph == 1 or al in (1, 2):
                faces_sent(ph, al)
    for al in range(4):
        pltpu.make_async_copy(sbuf.at[al, 0:15], sbuf.at[al, 0:15], tsend.at[al]).wait()
    pltpu.make_async_copy(idl.at[0:15], idl.at[0:15], isend).wait()
    for to, back, c in rims:
        pl.when(to)(c.wait_send)


def last_kernel(first, base, p2, out, rows32, buf, sems):
    copies = []
    for n, (yl, x0, m) in enumerate(((0, 0, 32), (1, 0, 32), (2, 0, 32), (3, 0, 16), (3, 16, 16))):
        xs = slice(x0, x0 + m)
        win = [
            first[yl + dy, x0 + dx : x0 + dx + m].reshape(16 * m, 256)
            for dy in range(3)
            for dx in range(3)
        ]
        s = mm(jnp.concatenate(win, axis=1), p2[...])
        s = s + base[yl, xs].reshape(16 * m, 256).astype(F32)
        for c in range(2):
            cs = slice(128 * c, 128 * c + 128)
            rows32[n % 2, c, 0 : 16 * m] = s[:, cs]
            for y in range(16):
                buf[yl, y, xs, cs] = rows32[n % 2, c, pl.ds(y, m, stride=16), :].astype(BF)
        c = pltpu.make_async_copy(buf.at[yl, :, xs], out.at[:, yl, xs], sems.at[n])
        c.start()
        copies.append(c)
    for c in copies:
        c.wait()


def local(
    features, links, block_slot, block_level, slot_column,
    conv_first, conv_second, height_w, plane_first, plane_second,
):
    hbm = pl.BlockSpec(memory_space=pltpu.HBM)
    vmem = pl.BlockSpec(memory_space=pltpu.VMEM)
    dma = pltpu.SemaphoreType.DMA
    operands = (
        features.reshape(8, 2, 4, 64, 128),
        links.T,
        block_slot,
        block_level,
        slot_column,
        conv_first.reshape(896, 128),
        conv_second.reshape(896, 128),
        height_w,
        plane_first.reshape(2304, 256),
    )
    first, base = pl.pallas_call(
        kernel,
        out_shape=[
            jax.ShapeDtypeStruct((6, 34, 16, 256), BF),
            jax.ShapeDtypeStruct((4, 32, 16, 256), BF),
        ],
        in_specs=[hbm] * 9,
        out_specs=[vmem, vmem],
        scratch_shapes=[
            pltpu.SMEM((3, 8), jnp.int32),
            pltpu.SMEM((8,), jnp.int32),
            pltpu.SMEM((8,), jnp.int32),
            pltpu.VMEM((1, 32), jnp.int32),
            pltpu.VMEM((8, 2, 4, 64, 128), BF),
            pltpu.VMEM((896, 128), BF),
            pltpu.VMEM((896, 128), BF),
            pltpu.VMEM((4, 1024, 256), BF),
            pltpu.VMEM((2304, 256), BF),
            pltpu.VMEM((6, 10, 10, 16, 128), BF),
            pltpu.VMEM((6, 10, 10, 16, 128), BF),
            pltpu.VMEM((2, 2, 4, 2, 8, 16, 128), BF),
            pltpu.VMEM((2, 2, 4, 2, 8, 16, 128), BF),
            pltpu.VMEM((2, 2, 64, 128), BF),
            pltpu.VMEM((2, 2, 64, 128), BF),
            pltpu.VMEM((2, 1024, 128), F32),
            pltpu.VMEM((4, 16, 32, 256), BF),
            pltpu.VMEM((4, 16, 32, 256), BF),
            pltpu.VMEM((1, 128), F32),
            pltpu.VMEM((16, 1, 128), F32),
            pltpu.VMEM((7, 36, 16, 256), BF),
            pltpu.VMEM((34, 8, 256), F32),
            pltpu.VMEM((3, 36, 8, 256), F32),
            pltpu.VMEM((2, 512, 128), F32),
            pltpu.VMEM((2, 2, 576, 128), F32),
            pltpu.VMEM((2, 4, 2, 16, 256), BF),
            pltpu.VMEM((2, 4, 2, 16, 256), BF),
            pltpu.VMEM((2, 2, 32, 256), BF),
            pltpu.VMEM((2, 2, 32, 256), BF),
            pltpu.VMEM((4, 2, 16, 256), BF),
            dma((12,)),
            dma((2, 2, 4)),
            dma((2, 2, 4)),
            dma((2, 2)),
            dma((2, 2)),
            dma((4,)),
            dma((4,)),
            dma,
            dma,
            dma((10,)),
            dma((10,)),
        ],
        compiler_params=pltpu.CompilerParams(
            collective_id=0, has_side_effects=True, vmem_limit_bytes=40 * 2**20
        ),
    )(
        *[pltpu.with_memory_space_constraint(x, pltpu.HBM) for x in operands]
    )
    out = pl.pallas_call(
        last_kernel,
        out_shape=jax.ShapeDtypeStruct((16, 4, 32, 256), BF),
        in_specs=[vmem, vmem, vmem],
        out_specs=hbm,
        scratch_shapes=[
            pltpu.VMEM((2, 2, 512, 128), F32),
            pltpu.VMEM((4, 16, 32, 256), BF),
            dma((5,)),
        ],
        compiler_params=pltpu.CompilerParams(vmem_limit_bytes=24 * 2**20),
    )(first, base, plane_second.reshape(2304, 256))
    return out.reshape(64, 32, 256)


def solution(mesh):
    in_specs = (
        P(("gy", "gx"), None, None),
        P(("gy", "gx"), None),
        P(("gy", "gx")),
        P(("gy", "gx")),
        P(("gy", "gx"), None),
        P(),
        P(),
        P(),
        P(),
        P(),
    )
    return jax.shard_map(
        local, mesh=mesh, in_specs=in_specs, out_specs=P("gy", "gx", None), check_vma=False
    )
```

```python
import jax
import jax.numpy as jnp
from jax import lax
from jax.experimental import pallas as pl
from jax.experimental.pallas import tpu as pltpu
from jax.sharding import PartitionSpec as P

NY = 8
NX = 16
MESH = pl.DeviceIdType.MESH
F32 = jnp.float32
BF = jnp.bfloat16


def iota(shape, dim):
    return lax.broadcasted_iota(jnp.int32, shape, dim)


def shr(x, n):
    return lax.shift_right_logical(x, jnp.int32(n))


def onehot(cond):
    return jnp.where(cond, 1.0, 0.0).astype(BF)


def mm(a, b):
    return jnp.dot(a, b, preferred_element_type=F32)


def halves(x):
    x = x.astype(F32)
    return x[:, 0:8], x[:, 8:16]


def one_up(x, last, scale=(1.0, 1.0)):
    low, high = (pltpu.roll(h, 7, 1) for h in halves(x))
    end = iota(low.shape, 1) == 7
    low = jnp.where(end, high, low) * scale[0]
    high = jnp.where(end, last, high * scale[1])
    return jnp.concatenate([low, high], axis=1).astype(BF)


def one_down(x, head, scale=(1.0, 1.0)):
    low, high = (pltpu.roll(h, 1, 1) for h in halves(x))
    end = iota(low.shape, 1) == 0
    high = jnp.where(end, low, high) * scale[1]
    low = jnp.where(end, head, low * scale[0])
    return jnp.concatenate([low, high], axis=1).astype(BF)


def kernel(
    x_hbm, links_hbm, slot_hbm, level_hbm, ids_hbm, w1_hbm, w2_hbm, h_hbm, p1_hbm,
    first, base,
    links, slot, level, ids_in, xv, w1, w2, hw, p1,
    fa, fb, stage, ghost, astage, aghost,
    rows32, sbuf, rbuf, ids, idl,
    bev, edge, win32, tile32, rim32, cstage, cland, rstage, rland, kland,
    wsem, hsend, hrecv, asend, arecv, tsend, trecv, isend, irecv, msend, mrecv,
):
    gy = lax.axis_index("gy")
    gx = lax.axis_index("gx")
    nxt = ((gy + (gx + 1) // NX) % NY, (gx + 1) % NX)
    prv = ((gy + NY - 1 + (gx + NX - 1) // NX) % NY, (gx + NX - 1) % NX)
    north, south = (gy + NY - 1) % NY, (gy + 1) % NY
    west, east = (gx + NX - 1) % NX, (gx + 1) % NX

    loads = [
        pltpu.make_async_copy(s, d, wsem.at[n])
        for n, (s, d) in enumerate(
            [
                *[(x_hbm.at[:, :, al], xv.at[:, :, al]) for al in (3, 0, 1, 2)],
                (w1_hbm, w1), (w2_hbm, w2), (h_hbm, hw), (p1_hbm, p1),
                (links_hbm, links), (slot_hbm, slot), (level_hbm, level), (ids_hbm, ids_in),
            ]
        )
    ]
    for load in loads:
        load.start()

    barrier = pltpu.get_barrier_semaphore()

    def hello(where):
        pl.semaphore_signal(barrier, inc=1, device_id=where, device_id_type=MESH)

    has_nxt = (gx < NX - 1) | (gy < NY - 1)
    has_prv = (gx > 0) | (gy > 0)
    can_n, can_s, can_w, can_e = gy > 0, gy < NY - 1, gx > 0, gx < NX - 1
    no = jnp.logical_not

    def greet(o, carry):
        hello((gy, (gx + o) % NX))
        return carry

    greeted = jnp.int32(NX - 1)
    for there, where in (
        (has_nxt, nxt),
        (has_prv, prv),
        (can_n, (north, gx)),
        (can_s, (south, gx)),
        (can_n & can_w, (north, west)),
        (can_n & can_e, (north, east)),
        (can_s & can_w, (south, west)),
        (can_s & can_e, (south, east)),
    ):
        greeted = greeted + there.astype(jnp.int32)

        @pl.when(there)
        def _(where=where):
            hello(where)

    lax.fori_loop(1, NX, greet, 0)

    for there, land in (
        (has_nxt, (ghost.at[:, 0], aghost.at[:, 0])),
        (has_prv, (ghost.at[:, 1], aghost.at[:, 1])),
        (can_e, (cland.at[0],)),
        (can_w, (cland.at[1],)),
        (can_s, (rland.at[0],)),
        (can_n, (rland.at[1],)),
        (can_s & can_e, (kland.at[0],)),
        (can_s & can_w, (kland.at[1],)),
        (can_n & can_e, (kland.at[2],)),
        (can_n & can_w, (kland.at[3],)),
    ):

        @pl.when(no(there))
        def _(land=land):
            for ref in land:
                ref[...] = jnp.zeros(ref.shape, BF)

    for load in loads[8:]:
        load.wait()
    ids[...] = jnp.zeros((1, 128), F32)
    ids[0:1, 0:32] = ids_in[...].astype(F32)

    s16 = iota((16, 128), 0)

    def per_block(read, index):
        m = jnp.zeros((16, 128), F32)
        for i in range(8):
            m = jnp.where(index == i, read(i).astype(F32), m)
        return m

    m1 = per_block(lambda i: links[1, i], shr(s16, 1))
    m2 = per_block(lambda i: links[2, i], shr(s16, 1))
    ma = jnp.where((s16 & 1) == 0, 1.0, per_block(lambda i: links[0, i], shr(s16, 1)))
    mb = jnp.where((s16 & 1) == 1, 1.0, per_block(lambda i: links[0, i], shr(s16, 1) - 1))
    top = links[0, 7].astype(F32)

    def times(x, m):
        return (x.astype(F32) * m).astype(BF)

    def face_copy(ph, way, al):
        return pltpu.make_async_remote_copy(
            src_ref=stage.at[ph, way, al],
            dst_ref=ghost.at[ph, way, al],
            send_sem=hsend.at[ph, way, al],
            recv_sem=hrecv.at[ph, way, al],
            device_id=nxt if way else prv,
            device_id_type=MESH,
        )

    def end_copy(ph, way):
        return pltpu.make_async_remote_copy(
            src_ref=astage.at[ph, way],
            dst_ref=aghost.at[ph, way],
            send_sem=asend.at[ph, way],
            recv_sem=arecv.at[ph, way],
            device_id=nxt if way else prv,
            device_id_type=MESH,
        )

    def ring(do, way, back=False):
        pl.when(has_nxt if (way == 1) != back else has_prv)(do)

    def send_faces(ph, al):
        for way in range(2):
            ring(lambda way=way: face_copy(ph, way, al).start(), way)

    def faces_sent(ph, al):
        for way in range(2):
            ring(lambda way=way: face_copy(ph, way, al).wait_send(), way)

    def lay_out(ph, arr, al):
        stage[ph, 0, al, 0] = arr[al + 1, 1, 1:9]
        stage[ph, 0, al, 1] = arr[al + 1, 1:9, 1]
        stage[ph, 1, al, 0] = times(arr[al + 1, 8, 1:9], m1)
        stage[ph, 1, al, 1] = times(arr[al + 1, 1:9, 8], m2)

    def send_end(ph, way):
        ring(lambda: end_copy(ph, way).start(), way)

    def absorb(ph, arr, al):
        for way in range(2):
            ring(lambda way=way: face_copy(ph, way, al).wait_recv(), way, True)
        arr[al + 1, 9, 1:9] = times(ghost[ph, 0, al, 0], m1)
        arr[al + 1, 1:9, 9] = times(ghost[ph, 0, al, 1], m2)
        arr[al + 1, 0, 1:9] = ghost[ph, 1, al, 0]
        arr[al + 1, 1:9, 0] = ghost[ph, 1, al, 1]

    def absorb_end(ph, arr, way):
        ring(lambda: end_copy(ph, way).wait_recv(), way, True)
        come = aghost[ph, way].astype(F32)
        rows32[way, pl.ds(0 if way else 15, 64, stride=16), :] = come if way else come * top
        for b in range(8):
            low, high = halves(rows32[way, b * 128 : b * 128 + 128].reshape(8, 16, 128))
            if way:
                arr[0, 1 + b, 1:9] = one_down(arr[4, 1 + b, 1:9], low, (mb[0:8], mb[8:16]))
            else:
                arr[5, 1 + b, 1:9] = one_up(arr[1, 1 + b, 1:9], high, (ma[0:8], ma[8:16]))

    def taps(arr, al, b0, nb):
        n = nb * 128
        win = [
            arr[al + 1, 1 + b0 : 1 + b0 + nb, 1:9],
            arr[al + 2, 1 + b0 : 1 + b0 + nb, 1:9],
            arr[al, 1 + b0 : 1 + b0 + nb, 1:9],
            arr[al + 1, 2 + b0 : 2 + b0 + nb, 1:9],
            arr[al + 1, b0 : b0 + nb, 1:9],
            arr[al + 1, 1 + b0 : 1 + b0 + nb, 2:10],
            arr[al + 1, 1 + b0 : 1 + b0 + nb, 0:8],
        ]
        return jnp.concatenate([w.reshape(n, 128) for w in win], axis=1)


    def send_ids(o, carry):
        pltpu.make_async_remote_copy(
            src_ref=ids,
            dst_ref=idl.at[gx],
            send_sem=isend,
            recv_sem=irecv,
            device_id=(gy, (gx + o) % NX),
            device_id_type=MESH,
        ).start()
        return carry

    def bring(t):
        al = (t + 3) % 4
        loads[t].wait()
        rows32[t % 2] = xv[:, :, al].reshape(1024, 128).astype(F32)
        for b in range(8):
            for c in range(8):
                cell = rows32[t % 2, pl.ds(8 * b + c, 16, stride=64), :]
                fa[al + 1, 1 + b, 1 + c] = cell.astype(BF)
        lay_out(0, fa, al)

    bring(0)
    astage[0, 1] = (xv[7, 1, 3].astype(F32) * top).astype(BF)
    bring(1)
    astage[0, 0] = xv[0, 0, 0]
    pl.semaphore_wait(barrier, greeted)
    send_end(0, 0)
    send_end(0, 1)
    send_faces(0, 3)
    send_faces(0, 0)
    bring(2)
    bring(3)
    idl[gx] = ids[...]
    faces_sent(0, 3)
    send_faces(0, 1)
    faces_sent(0, 0)
    send_faces(0, 2)

    loads[4].wait()
    absorb_end(0, fa, 0)
    absorb_end(0, fa, 1)

    for t in range(4):
        al = (t + 3) % 4
        absorb(0, fa, al)
        for b0 in (0, 4):
            h = jnp.maximum(mm(taps(fa, al, b0, 4), w1[...]), 0.0)
            fb[al + 1, 1 + b0 : 5 + b0, 1:9] = h.astype(BF).reshape(4, 8, 16, 128)
            if t < 2:
                rows32[t, b0 * 128 : b0 * 128 + 512] = h
        if t == 0:
            astage[1, 1] = (rows32[0, pl.ds(15, 64, stride=16), :] * top).astype(BF)
            send_end(1, 1)
        if t == 1:
            astage[1, 0] = rows32[1, pl.ds(0, 64, stride=16), :].astype(BF)
            send_end(1, 0)
        lay_out(1, fb, al)
        send_faces(1, al)

    lax.fori_loop(1, NX, send_ids, 0)

    lane = iota((1, 128), 1)
    slot_lane = jnp.zeros((1, 128), jnp.int32)
    for i in range(8):
        slot_lane = jnp.where((shr(lane, 1) & 7) == i, slot[i], slot_lane)
    slot_lane = jnp.concatenate([slot_lane, slot_lane], axis=1)
    k = iota((512, 256), 0)
    rho = iota((512, 256), 1) & 127
    slot_mat = onehot(
        (shr(k, 4) == slot_lane) & ((shr(k, 1) & 7) == shr(rho, 4)) & ((k & 1) == (rho & 1))
    )
    row_block = shr(iota((128, 256), 0), 1) & 7
    row_level = jnp.zeros((128, 256), jnp.int32)
    for i in range(8):
        row_level = jnp.where(row_block == i, level[i], row_level)

    loads[5].wait()
    loads[6].wait()

    def column_copy(al, o):
        to = (gx + o) % NX
        return pltpu.make_async_remote_copy(
            src_ref=sbuf.at[al, to],
            dst_ref=rbuf.at[al, gx],
            send_sem=tsend.at[al],
            recv_sem=trecv.at[al],
            device_id=(gy, to),
            device_id_type=MESH,
        )

    for t in range(4):
        al = (t + 3) % 4
        if t < 2:
            absorb_end(1, fb, t)
        absorb(1, fb, al)
        parts = []
        for b0 in (0, 4):
            v = mm(taps(fb, al, b0, 4), w2[...])
            v = v + fa[al + 1, 1 + b0 : 5 + b0, 1:9].reshape(512, 128).astype(F32)
            v = jnp.maximum(v, 0.0).astype(BF).reshape(4, 8, 16, 128)
            parts.append(
                jnp.concatenate([v[:, c].reshape(64, 128) for c in range(8)], axis=1)
            )
        rows = jnp.concatenate(parts, axis=0)
        lifted = jnp.zeros((128, 256), F32)
        for lv in range(4):
            lifted = jnp.where(row_level == lv, mm(rows, hw[lv]), lifted)
        high = lifted.astype(BF)
        low = (lifted - high.astype(F32)).astype(BF)
        sums = mm(slot_mat, jnp.concatenate([high, low], axis=0))
        sbuf[al] = sums.astype(BF).reshape(16, 32, 256)

        def send(o, c, al=al):
            column_copy(al, o).start()
            return c

        lax.fori_loop(1, NX, send, 0)
        rbuf[al, gx] = sbuf[al, gx]

    pltpu.make_async_copy(idl.at[0:15], idl.at[0:15], irecv).wait()
    sel = onehot(iota((128, 512), 0) == 2 * gx + (shr(iota((128, 512), 1), 4) & 1))
    got = mm(idl[...].reshape(16, 128).astype(BF), sel)
    got = jnp.where(iota((16, 512), 0) == shr(iota((16, 512), 1), 5), got, 0.0)
    cid = jnp.sum(got, axis=0, keepdims=True)
    r = iota((512, 512), 0)
    k = iota((512, 512), 1)
    want = (shr(r, 1) & 7) * 4 + shr(r, 7)
    tile_mat = onehot(
        (cid == want.astype(F32)) & ((shr(r, 4) & 7) == (shr(k, 1) & 7)) & ((r & 1) == (k & 1))
    )

    has_n = jnp.where(gy > 0, 1.0, 0.0).astype(F32)
    has_s = jnp.where(gy < NY - 1, 1.0, 0.0).astype(F32)
    has_w = jnp.where(gx > 0, 1.0, 0.0).astype(F32)
    has_e = jnp.where(gx < NX - 1, 1.0, 0.0).astype(F32)

    def rim(n, src, dst, where):
        return pltpu.make_async_remote_copy(
            src_ref=src,
            dst_ref=dst,
            send_sem=msend.at[n],
            recv_sem=mrecv.at[n],
            device_id=where,
            device_id_type=MESH,
        )

    early = [
        (can_w, can_e, rim(0, cstage.at[0, 0:3], cland.at[0, 0:3], (gy, west))),
        (can_e, can_w, rim(1, cstage.at[1, 0:3], cland.at[1, 0:3], (gy, east))),
        (can_n, can_s, rim(2, rstage.at[0], rland.at[0], (north, gx))),
        (can_n & can_w, can_s & can_e, rim(3, rstage.at[0, :, 0:16], kland.at[0], (north, west))),
        (can_n & can_e, can_s & can_w, rim(4, rstage.at[0, :, 16:32], kland.at[1], (north, east))),
    ]
    late = [
        (can_w, can_e, rim(5, cstage.at[0, 3:4], cland.at[0, 3:4], (gy, west))),
        (can_e, can_w, rim(6, cstage.at[1, 3:4], cland.at[1, 3:4], (gy, east))),
        (can_s, can_n, rim(7, rstage.at[1], rland.at[1], (south, gx))),
        (can_s & can_w, can_n & can_e, rim(8, rstage.at[1, :, 0:16], kland.at[2], (south, west))),
        (can_s & can_e, can_n & can_w, rim(9, rstage.at[1, :, 16:32], kland.at[3], (south, east))),
    ]
    rims = early + late

    def carry_down(arr, dst, src, x0, n):
        arr[dst, x0 : x0 + n] = one_down(arr[src, x0 : x0 + n], 0.0)

    def carry_up(arr, dst, src, x0, n):
        arr[dst, x0 : x0 + n] = one_up(arr[src, x0 : x0 + n], 0.0)

    def plane_inner(yl):
        win = [
            bev[yl + 1 + dy, 2 + dx : 32 + dx].reshape(480, 256)
            for dy in range(3)
            for dx in range(3)
        ]
        f = mm(jnp.concatenate(win, axis=1), p1[...])
        first[yl + 1, 2:32] = jnp.maximum(f, 0.0).astype(BF).reshape(30, 16, 256)

    for t in range(4):
        al = (t + 3) % 4
        pltpu.make_async_copy(rbuf.at[al, 0:15], rbuf.at[al, 0:15], trecv.at[al]).wait()
        tile = mm(tile_mat, rbuf[al].reshape(512, 256))
        bev[al + 2, 2:34] = tile.astype(BF).reshape(32, 16, 256)
        for c in range(2):
            cs = slice(128 * c, 128 * c + 128)
            tile32[c] = tile[:, cs]
            edge_rows = tile32[c, pl.ds(0 if al < 2 else 15, 32, stride=16), :]
            rstage[al // 2, al % 2, :, cs] = edge_rows.astype(BF)
        cstage[0, t] = bev[al + 2, 2:4]
        cstage[1, t] = bev[al + 2, 32:34]
        if t == 2:
            for to, back, c in early:
                pl.when(to)(c.start)
            loads[7].wait()
            carry_down(bev, 1, 5, 2, 32)
            plane_inner(0)
        if t == 3:
            for to, back, c in late:
                pl.when(to)(c.start)
            carry_up(bev, 6, 2, 2, 32)
            for yl in (3, 1, 2):
                plane_inner(yl)
            carry_down(first, 0, 4, 2, 30)
            carry_up(first, 5, 1, 2, 30)

    for to, back, c in rims:
        pl.when(back)(c.wait_recv)
    for t in range(4):
        al = (t + 3) % 4
        bev[al + 2, 34:36] = cland[0, t]
        bev[al + 2, 0:2] = cland[1, t]
    for x0 in (0, 34):
        carry_down(bev, 1, 5, x0, 2)
        carry_up(bev, 6, 2, x0, 2)
    for n in range(2):
        for c in range(2):
            cs = slice(128 * c, 128 * c + 128)
            for sub, way in ((0, 1), (15, 0)):
                rim32[n, c, pl.ds(32 + sub, 32, stride=16), :] = rland[way, n, :, cs].astype(F32)
                corner = kland[2 * way + 1, n, :, cs].astype(F32)[14:16]
                rim32[n, c, pl.ds(sub, 2, stride=16), :] = corner
                corner = kland[2 * way, n, :, cs].astype(F32)[0:2]
                rim32[n, c, pl.ds(544 + sub, 2, stride=16), :] = corner

    def map_half(slab, half):
        hs = slice(8 * half, 8 * half + 8)
        if slab in (0, 7):
            both = [rim32[slab // 7, c].reshape(36, 16, 128)[:, hs] for c in range(2)]
            return jnp.concatenate(both, axis=2)
        return bev[slab].astype(F32)[:, hs]

    s8 = iota((36, 8, 256), 1)
    for dy in range(3):
        top0, top1 = ((0, 7), (7, 2), (2, 3))[dy]
        low0, low1 = ((4, 5), (5, 0), (0, 7))[dy]
        upper = jnp.where(s8 == 0, map_half(top0, 0), pltpu.roll(map_half(top1, 0), 1, 1))
        lower = jnp.where(s8 == 7, map_half(low1, 1), pltpu.roll(map_half(low0, 1), 7, 1))
        win32[dy] = jnp.where(s8 < 2, upper, jnp.where(s8 > 5, lower, 0.0))
    win = [
        win32[dy, dx : dx + 34].reshape(272, 256).astype(BF) for dy in range(3) for dx in range(3)
    ]
    f = mm(jnp.concatenate(win, axis=1), p1[...])
    edge[...] = jnp.maximum(f, 0.0).reshape(34, 8, 256)
    win = [
        jnp.concatenate(
            [
                bev[1 + dy : 5 + dy, x0 + dx : x0 + dx + 2].reshape(128, 256) for x0 in (0, 32)
            ],
            axis=0,
        )
        for dy in range(3)
        for dx in range(3)
    ]
    f = mm(jnp.concatenate(win, axis=1), p1[...])
    f = jnp.maximum(f, 0.0).reshape(2, 4, 2, 16, 256)
    first[1:5, 0:1] = (f[0, :, 0:1] * has_w).astype(BF)
    first[1:5, 1:2] = f[0, :, 1:2].astype(BF)
    first[1:5, 32:33] = f[1, :, 0:1].astype(BF)
    first[1:5, 33:34] = (f[1, :, 1:2] * has_e).astype(BF)
    edge[0:1] = edge[0:1] * has_w
    edge[33:34] = edge[33:34] * has_e
    for x0 in (0, 32):
        carry_down(first, 0, 4, x0, 2)
        carry_up(first, 5, 1, x0, 2)
    s8 = iota((34, 8, 256), 1)
    rows = edge[...]

    def patch(slab, half, row, new):
        old = first[slab]
        keep = old[:, 0:8].astype(F32), old[:, 8:16].astype(F32)
        mixed = jnp.where(s8 == row, new, keep[half])
        both = [mixed, keep[1]] if half == 0 else [keep[0], mixed]
        first[slab] = jnp.concatenate(both, axis=1).astype(BF)

    patch(0, 0, 0, rows * has_n)
    patch(1, 0, 0, pltpu.roll(rows, 7, 1))
    patch(4, 1, 7, pltpu.roll(rows, 1, 1))
    patch(5, 1, 7, rows * has_s)
    base[...] = bev[2:6, 2:34]

    for ph in range(2):
        for way in range(2):
            ring(lambda ph=ph, way=way: end_copy(ph, way).wait_send(), way)
        for al in range(4):
            if ph == 1 or al in (1, 2):
                faces_sent(ph, al)
    for al in range(4):
        pltpu.make_async_copy(sbuf.at[al, 0:15], sbuf.at[al, 0:15], tsend.at[al]).wait()
    pltpu.make_async_copy(idl.at[0:15], idl.at[0:15], isend).wait()
    for to, back, c in rims:
        pl.when(to)(c.wait_send)


def last_kernel(first, base, p2, out, rows32, buf, sems):
    copies = []
    for n, (yl, x0, m) in enumerate(((0, 0, 32), (1, 0, 32), (2, 0, 32), (3, 0, 16), (3, 16, 16))):
        xs = slice(x0, x0 + m)
        win = [
            first[yl + dy, x0 + dx : x0 + dx + m].reshape(16 * m, 256)
            for dy in range(3)
            for dx in range(3)
        ]
        s = mm(jnp.concatenate(win, axis=1), p2[...])
        s = s + base[yl, xs].reshape(16 * m, 256).astype(F32)
        for c in range(2):
            cs = slice(128 * c, 128 * c + 128)
            rows32[n % 2, c, 0 : 16 * m] = s[:, cs]
            for y in range(16):
                buf[yl, y, xs, cs] = rows32[n % 2, c, pl.ds(y, m, stride=16), :].astype(BF)
        c = pltpu.make_async_copy(buf.at[yl, :, xs], out.at[:, yl, xs], sems.at[n])
        c.start()
        copies.append(c)
    for c in copies:
        c.wait()


def local(
    features, links, block_slot, block_level, slot_column,
    conv_first, conv_second, height_w, plane_first, plane_second,
):
    hbm = pl.BlockSpec(memory_space=pltpu.HBM)
    vmem = pl.BlockSpec(memory_space=pltpu.VMEM)
    dma = pltpu.SemaphoreType.DMA
    operands = (
        features.reshape(8, 2, 4, 64, 128),
        links.T,
        block_slot,
        block_level,
        slot_column,
        conv_first.reshape(896, 128),
        conv_second.reshape(896, 128),
        height_w,
        plane_first.reshape(2304, 256),
    )
    first, base = pl.pallas_call(
        kernel,
        out_shape=[
            jax.ShapeDtypeStruct((6, 34, 16, 256), BF),
            jax.ShapeDtypeStruct((4, 32, 16, 256), BF),
        ],
        in_specs=[hbm] * 9,
        out_specs=[vmem, vmem],
        scratch_shapes=[
            pltpu.SMEM((3, 8), jnp.int32),
            pltpu.SMEM((8,), jnp.int32),
            pltpu.SMEM((8,), jnp.int32),
            pltpu.VMEM((1, 32), jnp.int32),
            pltpu.VMEM((8, 2, 4, 64, 128), BF),
            pltpu.VMEM((896, 128), BF),
            pltpu.VMEM((896, 128), BF),
            pltpu.VMEM((4, 1024, 256), BF),
            pltpu.VMEM((2304, 256), BF),
            pltpu.VMEM((6, 10, 10, 16, 128), BF),
            pltpu.VMEM((6, 10, 10, 16, 128), BF),
            pltpu.VMEM((2, 2, 4, 2, 8, 16, 128), BF),
            pltpu.VMEM((2, 2, 4, 2, 8, 16, 128), BF),
            pltpu.VMEM((2, 2, 64, 128), BF),
            pltpu.VMEM((2, 2, 64, 128), BF),
            pltpu.VMEM((2, 1024, 128), F32),
            pltpu.VMEM((4, 16, 32, 256), BF),
            pltpu.VMEM((4, 16, 32, 256), BF),
            pltpu.VMEM((1, 128), F32),
            pltpu.VMEM((16, 1, 128), F32),
            pltpu.VMEM((7, 36, 16, 256), BF),
            pltpu.VMEM((34, 8, 256), F32),
            pltpu.VMEM((3, 36, 8, 256), F32),
            pltpu.VMEM((2, 512, 128), F32),
            pltpu.VMEM((2, 2, 576, 128), F32),
            pltpu.VMEM((2, 4, 2, 16, 256), BF),
            pltpu.VMEM((2, 4, 2, 16, 256), BF),
            pltpu.VMEM((2, 2, 32, 256), BF),
            pltpu.VMEM((2, 2, 32, 256), BF),
            pltpu.VMEM((4, 2, 16, 256), BF),
            dma((12,)),
            dma((2, 2, 4)),
            dma((2, 2, 4)),
            dma((2, 2)),
            dma((2, 2)),
            dma((4,)),
            dma((4,)),
            dma,
            dma,
            dma((10,)),
            dma((10,)),
        ],
        compiler_params=pltpu.CompilerParams(
            collective_id=0, has_side_effects=True, vmem_limit_bytes=40 * 2**20
        ),
    )(
        *[pltpu.with_memory_space_constraint(x, pltpu.HBM) for x in operands]
    )
    out = pl.pallas_call(
        last_kernel,
        out_shape=jax.ShapeDtypeStruct((16, 4, 32, 256), BF),
        in_specs=[vmem, vmem, vmem],
        out_specs=hbm,
        scratch_shapes=[
            pltpu.VMEM((2, 2, 512, 128), F32),
            pltpu.VMEM((4, 16, 32, 256), BF),
            dma((5,)),
        ],
        compiler_params=pltpu.CompilerParams(vmem_limit_bytes=24 * 2**20),
    )(first, base, plane_second.reshape(2304, 256))
    return out.reshape(64, 32, 256)


def solution(mesh):
    in_specs = (
        P(("gy", "gx"), None, None),
        P(("gy", "gx"), None),
        P(("gy", "gx")),
        P(("gy", "gx")),
        P(("gy", "gx"), None),
        P(),
        P(),
        P(),
        P(),
        P(),
    )
    return jax.shard_map(
        local, mesh=mesh, in_specs=in_specs, out_specs=P("gy", "gx", None), check_vma=False
    )
```
